256 devices in a mesh: period: 4 (over y), cont: 64 (over x, z, core).
Axes of the slice: x: 4, y: 4, z: 8, core: 2. Of those that a mesh axis runs over, the one named last changes fastest.
Arguments:
- factors: bfloat16 [4, 64, 2048, 128], P('period', 'cont'), may hold values from -0.125 to 0.125
- pattern: int32 [4, 64, 16], P('period', 'cont'), may hold values 0 or 1
- hessian: float32 [4, 2048], P('period', 'cont'), may hold values from 0.5 to 4
- ramp_map: bfloat16 [4, 2048, 1024], P('period'), may hold values from -0.125 to 0.125
Outputs:
- schur: float32 [4, 2048, 2048], P('period', 'cont')
- condensed: float32 [1024, 1024], P('period')
The draws below stay inside these ranges and needn't reach their ends.
All inputs are finite; a program needn't handle non-finite values. No bound on the sum of `pattern` on one device may be relied on, other than what follows from the above.
Results may differ from the reference program's by a relative error of at most 0.0003.
Values sent between devices are 32-bit elements; how exact they have to be, the bound alone decides.
No kernel may reach another device: no remote copies, remote signals or barrier semaphores. Data moves between devices by JAX's collectives and lax.ppermute only.
A program may use at most 128 MiB of HBM per device.

```python
import math
import jax
import jax.numpy as jnp
from jax import lax

NV = 2048
R = 128
IFACE = 1024
NBLK = 16
CONT = 64
PERIODS = 4


def plant(drawn, stream_key, low, high):
    place = [jax.random.randint(jax.random.fold_in(stream_key, axis), (), 0, length) for axis, length in enumerate(drawn.shape)]
    main_axis = drawn.shape.index(max(drawn.shape))
    next_to = place[:main_axis] + [(place[main_axis] + 1) % drawn.shape[main_axis]] + place[main_axis + 1:]
    return drawn.at[tuple(place)].set(low).at[tuple(next_to)].set(high)


def shard_levels(stream_key, shape, shards, least, top_value):
    factor_of = 1.0
    for position, blocks in shards:
        steps = jax.random.uniform(jax.random.fold_in(jax.random.fold_in(stream_key, 6), position), (blocks,), jnp.float32, least / len(shards), top_value / len(shards))
        factor_of = factor_of * jnp.repeat(jnp.exp(steps), shape[position] // blocks).reshape((-1,) + (1,) * (len(shape) - 1 - position))
    return factor_of


def centred(own_key, extent, spread, most, pieces=(), held_as=jnp.bfloat16):
    values = spread * jax.random.normal(own_key, extent, jnp.float32)
    if pieces:
        values = values * shard_levels(own_key, extent, pieces, -0.22, 0.18)
    return jnp.clip(values, -most, most).astype(held_as)


def setup_inputs(seed: int = 0) -> dict:
    keys = jax.random.split(jax.random.key(seed), 5)
    factors = centred(keys[0], (PERIODS, CONT, NV, R), (R * CONT // 4) ** -0.5, 0.125, ((0, 4), (1, 64)))
    pattern = plant((jax.random.randint(keys[1], (PERIODS, CONT, NBLK), 0, 4) < 3).astype(jnp.int32), jax.random.fold_in(keys[1], 1), 0, 1)
    hessian = jnp.clip(jnp.exp(math.log(4.0) - 2.0794415 * jax.random.uniform(keys[2], (PERIODS, NV), jnp.float32) ** shard_levels(keys[2], (PERIODS, NV), ((0, 4), (1, 64)), -0.2, 0.2)), 0.5, 4.0)
    ramp_map = centred(keys[3], (PERIODS, NV, IFACE), NV ** -0.5, 0.125, ((0, 4),))
    return {"factors": factors, "pattern": pattern, "hessian": hessian, "ramp_map": ramp_map}


def join(first, second):
    highest = lax.Precision.HIGHEST
    half = first.shape[0] // 2
    top_one = first[:half, :half]
    cross_one = first[:half, half:]
    bottom_one = first[half:, half:]
    top_two = second[:half, :half]
    cross_two = second[:half, half:]
    bottom_two = second[half:, half:]
    lower = jnp.linalg.cholesky(bottom_one + top_two)
    stacked = jnp.concatenate([cross_one.T, cross_two], axis=1)
    solved = jax.scipy.linalg.solve_triangular(lower, stacked, lower=True)
    left_part = solved[:, :half]
    right_part = solved[:, half:]
    new_top = top_one - jnp.dot(left_part.T, left_part, precision=highest)
    new_cross = -jnp.dot(left_part.T, right_part, precision=highest)
    new_bottom = bottom_two - jnp.dot(right_part.T, right_part, precision=highest)
    upper_rows = jnp.concatenate([new_top, new_cross], axis=1)
    lower_rows = jnp.concatenate([new_cross.T, new_bottom], axis=1)
    return jnp.concatenate([upper_rows, lower_rows], axis=0)

def reference(factors, pattern, hessian, ramp_map):
    highest = lax.Precision.HIGHEST
    schur_list = []
    block_list = []
    for period_id in range(PERIODS):
        present = jnp.repeat(pattern[period_id], R, axis=1).astype(jnp.float32)
        masked = factors[period_id].astype(jnp.float32) * present[:, :, None]
        summed = lax.dot_general(masked, masked, (((0, 2), (0, 2)), ((), ())), precision=highest)
        schur_block = summed + jnp.diag(hessian[period_id])
        ramp = ramp_map[period_id].astype(jnp.float32)
        image = jnp.dot(schur_block, ramp, precision=highest)
        block_list.append(jnp.dot(ramp.T, image, precision=highest))
        schur_list.append(schur_block)
    condensed = block_list[0]
    for period_id in range(1, PERIODS):
        condensed = join(condensed, block_list[period_id])
    return (jnp.stack(schur_list), condensed)
```

```python
import functools
import jax
import jax.numpy as jnp
from jax import lax
from jax.experimental import pallas as pl
from jax.experimental.pallas import tpu as pltpu
from jax.sharding import Mesh, PartitionSpec as P

HIGHEST = lax.Precision.HIGHEST
BLOCK = 128
PIVOT = 4
CONT_AXES = ("x", "z", "core")


def invert_blocks(blocks):
    lane = lax.broadcasted_iota(jnp.int32, (1, BLOCK), 1)
    sub = lax.broadcasted_iota(jnp.int32, (BLOCK, 1), 0)
    for k in range(0, BLOCK, PIVOT):
        span = range(PIVOT)
        stepped = []
        for a in blocks:
            rows = [a[k + i : k + i + 1, :] for i in span]
            cols = [a[:, k + i : k + i + 1] for i in span]
            s = [
                [jnp.broadcast_to(a[k + i : k + i + 1, k + j : k + j + 1], (1, BLOCK)) for j in span]
                for i in span
            ]
            for t in span:
                ip = 1.0 / s[t][t]
                r = [s[t][j] * ip if j != t else ip for j in span]
                for i in span:
                    if i == t:
                        continue
                    c = s[i][t]
                    s[i] = [s[i][j] - c * r[j] if j != t else -c * ip for j in span]
                s[t] = r
            lane_in = (lane >= k) & (lane < k + PIVOT)
            sub_in = (sub >= k) & (sub < k + PIVOT)
            ident = [jnp.where(lane == k + i, 1.0, jnp.where(lane_in, 0.0, rows[i])) for i in span]
            new_rows = [sum(s[i][j] * ident[j] for j in span) for i in span]
            a = jnp.where(lane_in | sub_in, 0.0, a)
            for i in span:
                col = jnp.where(sub == k + i, -1.0, jnp.where(sub_in, 0.0, cols[i]))
                a = a - col * new_rows[i]
            stepped.append(a)
        blocks = stepped
    return blocks


def mm(a, b):
    return jnp.dot(a, b, precision=HIGHEST, preferred_element_type=jnp.float32)


def inverse_kernel(m_ref, o_ref):
    count, size, _ = m_ref.shape
    o_ref[...] = m_ref[...]

    def step(k, carry):
        off = pl.multiple_of(k * BLOCK, BLOCK)
        here = pl.ds(off, BLOCK)
        inv = invert_blocks([o_ref[b, here, here] for b in range(count)])
        col_id = lax.broadcasted_iota(jnp.int32, (1, size), 1)
        row_id = lax.broadcasted_iota(jnp.int32, (size, 1), 0)
        col_in = (col_id >= off) & (col_id < off + BLOCK)
        row_in = (row_id >= off) & (row_id < off + BLOCK)
        for b in range(count):
            cols = jnp.where(row_in, 0.0, o_ref[b, :, here])
            rows = mm(inv[b], jnp.where(col_in, 0.0, o_ref[b, here, :]))
            o_ref[b] = o_ref[b] - mm(cols, rows)
            o_ref[b, :, here] = -mm(cols, inv[b])
            o_ref[b, here, :] = rows
            o_ref[b, here, here] = inv[b]
        return carry

    lax.fori_loop(0, size // BLOCK, step, 0)


def inverse(m):
    count, size, _ = m.shape
    return pl.pallas_call(
        inverse_kernel,
        out_shape=jax.ShapeDtypeStruct(m.shape, jnp.float32),
        in_specs=[pl.BlockSpec(memory_space=pltpu.VMEM)],
        out_specs=pl.BlockSpec(memory_space=pltpu.VMEM),
        compiler_params=pltpu.CompilerParams(vmem_limit_bytes=32 << 20),
        cost_estimate=pl.CostEstimate(
            flops=count * 12 * size**3, bytes_accessed=count * 8 * size**2, transcendentals=0
        ),
    )(m)


def exchange(v, axis):
    return lax.all_to_all(v, axis, 0, 0, tiled=True)


def gather(v, axis):
    return exchange(jnp.broadcast_to(v[None], (lax.axis_size(axis),) + v.shape), axis)


def scatter_sum(v):
    rows, width = v.shape
    per = rows // 64
    v = v.reshape(2, rows // 2, width)
    core = lax.axis_index("core")
    other = lax.ppermute(lax.dynamic_index_in_dim(v, 1 - core, 0, False), "core", [(0, 1), (1, 0)])
    v = lax.dynamic_index_in_dim(v, core, 0, False) + other
    v = jnp.sum(exchange(v.reshape(4, rows // 8, width), "x"), axis=0)
    return jnp.sum(exchange(v.reshape(8, per, width), "z"), axis=0)


def gather_rows(v):
    per, width = v.shape
    v = gather(v, "z").reshape(8 * per, width)
    v = gather(v, "x").reshape(32 * per, width)
    other = lax.ppermute(v, "core", [(0, 1), (1, 0)])
    core = lax.axis_index("core")
    first = jnp.where(core == 0, v, other)
    second = jnp.where(core == 0, other, v)
    return jnp.concatenate([first, second], axis=0)


def on_device(factors, pattern, hessian, ramp_map):
    factor = factors[0, 0]
    nv, block_rows = factor.shape
    present = jnp.repeat(pattern[0, 0], block_rows).astype(jnp.bfloat16)
    masked = factor * present[:, None]
    rows = hessian.shape[1]
    position = (lax.axis_index("x") * 8 + lax.axis_index("z")) * 2 + lax.axis_index("core")
    start = position * rows
    ramp = ramp_map[0]
    iface = ramp.shape[1]
    half = iface // 2

    with jax.named_scope("interface_partial"):
        image = lax.dot_general(ramp, masked, (((0,), (0,)), ((), ())), preferred_element_type=jnp.float32)
        ramp_rows = lax.dynamic_slice_in_dim(ramp, start, rows, 0).astype(jnp.float32)
        left = jnp.concatenate([image, (ramp_rows * hessian[0][:, None]).T], axis=1)
        right = jnp.concatenate([image, ramp_rows.T], axis=1)
        top = mm(left[:half], right.T)
        low = mm(left[half:], right[half:].T)
        diag_part = jnp.concatenate([top[:, :half], low], axis=1)
        cross_part = top[:, half:]

    with jax.named_scope("diag_sum"):
        diag_rows = scatter_sum(diag_part)
        diag_all = gather(diag_rows, "period")
        tops, bottoms = diag_all[:, :, :half], diag_all[:, :, half:]
        m1 = bottoms[0] + tops[1]
        m2 = bottoms[1] + tops[2]
        m3 = bottoms[2] + tops[3]
        m13 = gather_rows(jnp.concatenate([m1, m3], axis=1))

    period = lax.axis_index("period")
    late = period >= 2
    with jax.named_scope("cross_sum"):
        cross_rows = scatter_sum(cross_part)
        cross_all = gather(cross_rows, "period")
        outer = jnp.where(late, bottoms[3], tops[0])
        rest = gather_rows(jnp.concatenate([cross_all[0], cross_all[1], cross_all[2], cross_all[3], m2, outer], axis=1))
        b0, b1, b2, b3, m2, outer = [rest[:, i * half : (i + 1) * half] for i in range(6)]

    with jax.named_scope("first_joins"):
        inv13 = inverse(jnp.stack([m13[:, :half], m13[:, half:]]))
        b3t = b3.T
        b2t = b2.T
        t1 = mm(inv13[0], b1)
        t3 = mm(inv13[1], b2t)
        middle = m2 - mm(b1.T, t1) - mm(b2, t3)
        c1 = -mm(b0, t1)
        c2t = -mm(b3t, t3)

    with jax.named_scope("last_join"):
        inv2 = inverse(middle[None])[0]
        quarter = half // 2
        off = (period % 2) * quarter
        edge = jnp.where(late, b3t, b0)
        edge_rows = lax.dynamic_slice_in_dim(edge, off, quarter, 0)
        inner = jnp.where(late, inv13[1], inv13[0])
        base = lax.dynamic_slice_in_dim(outer, off, quarter, 0) - mm(mm(edge_rows, inner), edge.T)
        c_rows = lax.dynamic_slice_in_dim(jnp.where(late, c2t, c1), off, quarter, 0)
        z = mm(c_rows, inv2)
        out_left = jnp.where(late, 0.0, base) - mm(z, c1.T)
        out_right = jnp.where(late, base, 0.0) - mm(z, c2t.T)
        my_rows = jnp.concatenate([out_left, out_right], axis=1)

    with jax.named_scope("schur"):
        partial_sum = lax.dot_general(masked, masked, (((1,), (1,)), ((), ())), preferred_element_type=jnp.float32)
        schur_rows = lax.psum_scatter(partial_sum, CONT_AXES, scatter_dimension=0, tiled=True)
        column_ids = lax.broadcasted_iota(jnp.int32, (rows, nv), 1)
        row_ids = lax.broadcasted_iota(jnp.int32, (rows, nv), 0) + start
        schur_rows = schur_rows + jnp.where(column_ids == row_ids, hessian[0][:, None], jnp.float32(0.0))
    return (schur_rows[None], my_rows)


def solution(mesh):
    fine = Mesh(mesh.devices.reshape(4, 4, 8, 2), ("period",) + CONT_AXES)
    in_specs = (
        P("period", CONT_AXES, None, None),
        P("period", CONT_AXES, None),
        P("period", CONT_AXES),
        P("period", None, None),
    )
    out_specs = (P("period", CONT_AXES, None), P("period", None))
    return jax.shard_map(on_device, mesh=fine, in_specs=in_specs, out_specs=out_specs, check_vma=False)
```

```python
import functools
import jax
import jax.numpy as jnp
from jax import lax
from jax.experimental import pallas as pl
from jax.experimental.pallas import tpu as pltpu
from jax.sharding import Mesh, PartitionSpec as P

HIGHEST = lax.Precision.HIGHEST
BLOCK = 128
PIVOT = 4
CONT_AXES = ("x", "z", "core")


def invert_blocks(blocks):
    lane = lax.broadcasted_iota(jnp.int32, (1, BLOCK), 1)
    sub = lax.broadcasted_iota(jnp.int32, (BLOCK, 1), 0)
    for k in range(0, BLOCK, PIVOT):
        span = range(PIVOT)
        stepped = []
        for a in blocks:
            rows = [a[k + i : k + i + 1, :] for i in span]
            cols = [a[:, k + i : k + i + 1] for i in span]
            s = [
                [jnp.broadcast_to(a[k + i : k + i + 1, k + j : k + j + 1], (1, BLOCK)) for j in span]
                for i in span
            ]
            for t in span:
                ip = 1.0 / s[t][t]
                r = [s[t][j] * ip if j != t else ip for j in span]
                for i in span:
                    if i == t:
                        continue
                    c = s[i][t]
                    s[i] = [s[i][j] - c * r[j] if j != t else -c * ip for j in span]
                s[t] = r
            lane_in = (lane >= k) & (lane < k + PIVOT)
            sub_in = (sub >= k) & (sub < k + PIVOT)
            ident = [jnp.where(lane == k + i, 1.0, jnp.where(lane_in, 0.0, rows[i])) for i in span]
            new_rows = [sum(s[i][j] * ident[j] for j in span) for i in span]
            a = jnp.where(lane_in | sub_in, 0.0, a)
            for i in span:
                col = jnp.where(sub == k + i, -1.0, jnp.where(sub_in, 0.0, cols[i]))
                a = a - col * new_rows[i]
            stepped.append(a)
        blocks = stepped
    return blocks


def mm(a, b):
    return jnp.dot(a, b, precision=HIGHEST, preferred_element_type=jnp.float32)


def tmm(a, b):
    dims = (((0,), (0,)), ((), ()))
    return lax.dot_general(a, b, dims, precision=HIGHEST, preferred_element_type=jnp.float32)


def inverse_step_kernel(k, m_ref, o_ref):
    size = m_ref.shape[0]
    off = k * BLOCK
    here = pl.ds(off, BLOCK)
    inv = invert_blocks([m_ref[here, here]])[0]
    col_id = lax.broadcasted_iota(jnp.int32, (1, size), 1)
    row_id = lax.broadcasted_iota(jnp.int32, (size, 1), 0)
    col_in = (col_id >= off) & (col_id < off + BLOCK)
    row_in = (row_id >= off) & (row_id < off + BLOCK)
    cols = jnp.where(row_in, 0.0, m_ref[:, here])
    rows = mm(inv, jnp.where(col_in, 0.0, m_ref[here, :]))
    o_ref[...] = m_ref[...] - mm(cols, rows)
    o_ref[:, here] = -mm(cols, inv)
    o_ref[here, :] = rows
    o_ref[here, here] = inv


def inverse(m):
    size = m.shape[0]
    for k in range(size // BLOCK):
        m = pl.pallas_call(
            functools.partial(inverse_step_kernel, k),
            out_shape=jax.ShapeDtypeStruct(m.shape, jnp.float32),
            in_specs=[pl.BlockSpec(memory_space=pltpu.VMEM)],
            out_specs=pl.BlockSpec(memory_space=pltpu.VMEM),
            compiler_params=pltpu.CompilerParams(vmem_limit_bytes=16 << 20),
            cost_estimate=pl.CostEstimate(
                flops=100 * size**3, bytes_accessed=8 * size**2, transcendentals=0
            ),
        )(m)
    return m


def gram_kernel(lhs_a, lhs_b, rhs_a, rhs_b, o_ref):
    dims = (((1,), (1,)), ((), ()))
    total = jnp.zeros(o_ref.shape, jnp.float32)
    for lhs, rhs in ((lhs_a, rhs_a), (lhs_b, rhs_b)):
        total = total + lax.dot_general(
            lhs[0].astype(jnp.bfloat16), rhs[0].astype(jnp.bfloat16), dims, preferred_element_type=jnp.float32
        )

    @pl.when(pl.program_id(0) == 0)
    def _():
        o_ref[...] = total

    @pl.when(pl.program_id(0) != 0)
    def _():
        o_ref[...] = o_ref[...] + total


def gram(lhs_a, lhs_b, rhs_a, rhs_b):
    steps, rows, depth = lhs_a.shape
    columns = rhs_a.shape[1]
    small = pl.BlockSpec((1, rows, depth), lambda i: (i, 0, 0))
    large = pl.BlockSpec((1, columns, depth), lambda i: (i, 0, 0))
    return pl.pallas_call(
        gram_kernel,
        grid=(steps,),
        out_shape=jax.ShapeDtypeStruct((rows, columns), jnp.float32),
        in_specs=[small, small, large, large],
        out_specs=pl.BlockSpec((rows, columns), lambda i: (0, 0)),
        compiler_params=pltpu.CompilerParams(vmem_limit_bytes=32 << 20),
        cost_estimate=pl.CostEstimate(
            flops=4 * steps * rows * columns * depth, bytes_accessed=8 * steps * columns * depth, transcendentals=0
        ),
    )(lhs_a, lhs_b, rhs_a, rhs_b)


def exchange(v, axis):
    return lax.all_to_all(v, axis, 0, 0, tiled=True)


def gather(v, axis):
    return exchange(jnp.broadcast_to(v[None], (lax.axis_size(axis),) + v.shape), axis)


def tie(v, *others):
    return lax.optimization_barrier((v,) + others)[0]


def other_core(v):
    return lax.ppermute(v, "core", [(0, 1), (1, 0)])


def partner(v, mask):
    return lax.ppermute(v, "period", [(i, i ^ mask) for i in range(4)])


def both_cores(v):
    other = other_core(v)
    first = lax.axis_index("core") == 0
    return jnp.concatenate([jnp.where(first, v, other), jnp.where(first, other, v)], axis=0)


def core_sum(v):
    rows, width = v.shape
    v = v.reshape(2, rows // 2, width)
    core = lax.axis_index("core")
    mine = lax.dynamic_index_in_dim(v, core, 0, False)
    return mine + other_core(lax.dynamic_index_in_dim(v, 1 - core, 0, False))


def axis_sum(v, axis):
    size = lax.axis_size(axis)
    return jnp.sum(exchange(v.reshape(size, v.shape[0] // size, v.shape[1]), axis), axis=0)


def axis_rows(v, axis):
    return gather(v, axis).reshape(lax.axis_size(axis) * v.shape[0], v.shape[1])


def on_device(factors, pattern, hessian, ramp_map):
    factor = factors[0, 0]
    nv, block_rows = factor.shape
    present = jnp.repeat(pattern[0, 0], block_rows).astype(jnp.bfloat16)
    masked = factor * present[:, None]
    rows = hessian.shape[1]
    core = lax.axis_index("core")
    x_at = lax.axis_index("x")
    start = ((x_at * 8 + lax.axis_index("z")) * 2 + core) * rows
    ramp = ramp_map[0]
    half = ramp.shape[1] // 2
    period = lax.axis_index("period")
    even = period % 2 == 0
    middle_period = (period == 1) | (period == 2)

    with jax.named_scope("interface_partial"):
        image = lax.dot_general(ramp, masked, (((0,), (0,)), ((), ())), preferred_element_type=jnp.float32)
        ramp_rows = lax.dynamic_slice_in_dim(ramp, start, rows, 0).astype(jnp.float32)
        left = jnp.concatenate([image, (ramp_rows * hessian[0][:, None]).T], axis=1)
        right = jnp.concatenate([image, ramp_rows.T], axis=1)
        inner_left = jnp.where(even, left[half:], left[:half])
        inner_right = jnp.where(even, right[half:], right[:half])
        outer_left = jnp.where(even, left[:half], left[half:])
        outer_right = jnp.where(even, right[:half], right[half:])
        inner = mm(inner_left, inner_right.T)
        cross = mm(inner_left, outer_right.T)
        outer = mm(outer_left, outer_right.T)

    with jax.named_scope("inner_sum"):
        inner = core_sum(inner)
        rest = core_sum(tie(jnp.concatenate([cross, outer], axis=1), inner))
        inner = axis_sum(inner, "x")
        rest = axis_sum(tie(rest, inner), "x")
        inner = axis_sum(inner, "z")
        rest = axis_sum(tie(rest, inner), "z")
        inner = inner + partner(inner, 1)
        rest_partner = partner(tie(rest, inner), 1)
        near = jnp.where(middle_period, rest, rest_partner)
        far = jnp.where(middle_period, rest_partner, rest)
        inner = axis_rows(inner, "z")
        near = axis_rows(tie(near, inner), "z")
        inner = axis_rows(inner, "x")
        near = axis_rows(tie(near, inner), "x")
        inner = both_cores(inner)
        near = both_cores(near)
        far = axis_rows(tie(far, near), "z")
        far = axis_rows(far, "x")
        far = both_cores(far)

    with jax.named_scope("schur_gather"):
        wide = lax.optimization_barrier(masked.astype(jnp.float32))
        mine = gather(wide, "x")
        other = other_core(mine)
        mine, other = lax.optimization_barrier((mine, other))

    with jax.named_scope("first_join"):
        inv1 = inverse(inner)
        t = mm(inv1, near[:, :half])
        kept = near[:, half:] - tmm(near[:, :half], t)
        kept_half = lax.dynamic_slice_in_dim(kept, core * (half // 2), half // 2, 0)
        kept_half = kept_half + partner(kept_half, 3)
        middle = both_cores(kept_half)
        c = -tmm(far[:, :half], t)
        c_half = partner(tie(lax.dynamic_slice_in_dim(c, core * (half // 2), half // 2, 0), kept_half), 3)
        c_other = both_cores(c_half)

    with jax.named_scope("schur_partial"):
        size = lax.axis_size("x")
        lhs = [
            lax.dynamic_slice(
                v.reshape(4, 4, 8, 2, rows, block_rows), (0, x_at, 0, core, 0, 0), (4, 1, 8, 1, rows, block_rows)
            ).reshape(size, 8 * rows, block_rows)
            for v in (mine, other)
        ]
        partial_sum = gram(lhs[0], lhs[1], mine, other)

    with jax.named_scope("last_join"):
        inv2 = inverse(middle)
        quarter = half // 2
        off = (period % 2) * quarter
        edge = far[:, :half]
        edge_cols = lax.dynamic_slice_in_dim(edge, off, quarter, 1)
        base = lax.dynamic_slice_in_dim(far[:, half:], off, quarter, 0) - mm(tmm(edge_cols, inv1), edge)
        z = mm(lax.dynamic_slice_in_dim(c, off, quarter, 0), inv2)
        out_own = base - mm(z, c.T)
        out_other = -mm(z, c_other.T)
        late = period >= 2
        my_rows = jnp.concatenate(
            [jnp.where(late, out_other, out_own), jnp.where(late, out_own, out_other)], axis=1
        )

    with jax.named_scope("schur_sum"):
        schur_rows = axis_sum(partial_sum, "z")
        column_ids = lax.broadcasted_iota(jnp.int32, (rows, nv), 1)
        row_ids = lax.broadcasted_iota(jnp.int32, (rows, nv), 0) + start
        schur_rows = schur_rows + jnp.where(column_ids == row_ids, hessian[0][:, None], jnp.float32(0.0))
    return (schur_rows[None], my_rows)


def solution(mesh):
    fine = Mesh(mesh.devices.reshape(4, 4, 8, 2), ("period",) + CONT_AXES)
    in_specs = (
        P("period", CONT_AXES, None, None),
        P("period", CONT_AXES, None),
        P("period", CONT_AXES),
        P("period", None, None),
    )
    out_specs = (P("period", CONT_AXES, None), P("period", None))
    return jax.shard_map(on_device, mesh=fine, in_specs=in_specs, out_specs=out_specs, check_vma=False)
```

```python
import functools
import jax
import jax.numpy as jnp
from jax import lax
from jax.experimental import pallas as pl
from jax.experimental.pallas import tpu as pltpu
from jax.sharding import Mesh, PartitionSpec as P

HIGHEST = lax.Precision.HIGHEST
BLOCK = 128
PIVOT = 4
CONT_AXES = ("x", "z", "core")


def invert_blocks(blocks):
    lane = lax.broadcasted_iota(jnp.int32, (1, BLOCK), 1)
    sub = lax.broadcasted_iota(jnp.int32, (BLOCK, 1), 0)
    for k in range(0, BLOCK, PIVOT):
        span = range(PIVOT)
        stepped = []
        for a in blocks:
            rows = [a[k + i : k + i + 1, :] for i in span]
            cols = [a[:, k + i : k + i + 1] for i in span]
            s = [
                [jnp.broadcast_to(a[k + i : k + i + 1, k + j : k + j + 1], (1, BLOCK)) for j in span]
                for i in span
            ]
            for t in span:
                ip = 1.0 / s[t][t]
                r = [s[t][j] * ip if j != t else ip for j in span]
                for i in span:
                    if i == t:
                        continue
                    c = s[i][t]
                    s[i] = [s[i][j] - c * r[j] if j != t else -c * ip for j in span]
                s[t] = r
            lane_in = (lane >= k) & (lane < k + PIVOT)
            sub_in = (sub >= k) & (sub < k + PIVOT)
            ident = [jnp.where(lane == k + i, 1.0, jnp.where(lane_in, 0.0, rows[i])) for i in span]
            new_rows = [sum(s[i][j] * ident[j] for j in span) for i in span]
            a = jnp.where(lane_in | sub_in, 0.0, a)
            for i in span:
                col = jnp.where(sub == k + i, -1.0, jnp.where(sub_in, 0.0, cols[i]))
                a = a - col * new_rows[i]
            stepped.append(a)
        blocks = stepped
    return blocks


def mm(a, b):
    return jnp.dot(a, b, precision=HIGHEST, preferred_element_type=jnp.float32)


def tmm(a, b):
    dims = (((0,), (0,)), ((), ()))
    return lax.dot_general(a, b, dims, precision=HIGHEST, preferred_element_type=jnp.float32)


def nt(a, b):
    dims = (((1,), (1,)), ((), ()))
    return lax.dot_general(a, b, dims, precision=HIGHEST, preferred_element_type=jnp.float32)


def pick(first, a, b):
    return jnp.where(first, a, b)


def turned(second, a):
    half = a.shape[1] // 2
    return jnp.where(second, jnp.concatenate([a[:, half:], a[:, :half]], axis=1), a)


def cut(rows):
    return jnp.concatenate([rows[:BLOCK, : 3 * BLOCK], rows[BLOCK:, BLOCK:]], axis=0)


def tile(half, row, place):
    return half[row * BLOCK : (row + 1) * BLOCK, place * BLOCK : (place + 1) * BLOCK]


def full_rows(here, there):
    top = jnp.concatenate([here[:BLOCK], tile(there, 1, 1).T], axis=1)
    low = jnp.concatenate([tile(here, 0, 1).T, here[BLOCK:]], axis=1)
    return jnp.concatenate([top, low], axis=0)


VMEM_SPEC = pl.BlockSpec(memory_space=pltpu.VMEM)
SMEM_SPEC = pl.BlockSpec(memory_space=pltpu.SMEM)


def f32(*shape):
    return jax.ShapeDtypeStruct(shape, jnp.float32)


def call(kernel, out_shape, scalars, arrays, flops):
    many = isinstance(out_shape, (list, tuple))
    moved = sum(a.size * a.dtype.itemsize for a in arrays)
    return pl.pallas_call(
        kernel,
        out_shape=out_shape,
        in_specs=[SMEM_SPEC] * len(scalars) + [VMEM_SPEC] * len(arrays),
        out_specs=[VMEM_SPEC] * len(out_shape) if many else VMEM_SPEC,
        compiler_params=pltpu.CompilerParams(vmem_limit_bytes=32 << 20),
        cost_estimate=pl.CostEstimate(flops=flops, bytes_accessed=moved, transcendentals=0),
    )(*scalars, *arrays)


def partial_kernel(flags, pattern, factor, ramp, hess, mine, theirs):
    even, core = flags[0] == 0, flags[1]
    start = pl.multiple_of(flags[2], 32)
    half = ramp.shape[1] // 2
    blocks = pattern.shape[0]
    masked = jnp.concatenate(
        [
            jnp.where(pattern[b] != 0, factor[b * BLOCK : (b + 1) * BLOCK, :], jnp.bfloat16(0))
            for b in range(blocks)
        ],
        axis=0,
    )
    image = lax.dot_general(masked, ramp[...], (((0,), (0,)), ((), ())), preferred_element_type=jnp.float32)
    ramp_rows = ramp[pl.ds(start, 32), :].astype(jnp.float32)
    left = jnp.concatenate([image, ramp_rows * hess[...]], axis=0)
    right = jnp.concatenate([image, ramp_rows], axis=0)
    inner_left = pick(even, left[:, half:], left[:, :half])
    inner_right = pick(even, right[:, half:], right[:, :half])
    outer_left = pick(even, left[:, :half], left[:, half:])
    outer_right = pick(even, right[:, :half], right[:, half:])
    for out, q in ((mine, core), (theirs, 1 - core)):
        inner_half = turned(q == 1, inner_left)[:, : half // 2]
        outer_half = turned(q == 1, outer_left)[:, : half // 2]
        out[:, :384] = cut(tmm(inner_half, turned(q == 1, inner_right)))
        out[:, 384:896] = tmm(inner_half, outer_right)
        out[:, 896:] = cut(tmm(outer_half, turned(q == 1, outer_right)))


def sweep(k, ref):
    size = ref.shape[0]
    off = k * BLOCK
    here = pl.ds(off, BLOCK)
    inv = invert_blocks([ref[here, here]])[0]
    col_id = lax.broadcasted_iota(jnp.int32, (1, size), 1)
    row_id = lax.broadcasted_iota(jnp.int32, (size, 1), 0)
    col_in = (col_id >= off) & (col_id < off + BLOCK)
    row_in = (row_id >= off) & (row_id < off + BLOCK)
    cols = jnp.where(row_in, 0.0, ref[:, here])
    rows = mm(inv, jnp.where(col_in, 0.0, ref[here, :]))
    ref[...] = ref[...] - mm(cols, rows)
    ref[:, here] = -mm(cols, inv)
    ref[here, :] = rows
    ref[here, here] = inv


def first_sweep_kernel(flags, own, other, o_ref):
    first = flags[1] == 0
    top = pick(first, own[...], other[...])
    low = pick(first, other[...], own[...])
    half = top.shape[0]
    o_ref[:half, :] = full_rows(top, low)
    low_rows = full_rows(low, top)
    o_ref[half:, :half] = low_rows[:, half:]
    o_ref[half:, half:] = low_rows[:, :half]
    sweep(0, o_ref)


def sweep_kernel(k, m_ref, o_ref):
    o_ref[...] = m_ref[...]
    sweep(k, o_ref)


def inverse(flags, own, other):
    size = 2 * own.shape[0]
    m = call(first_sweep_kernel, f32(size, size), [flags], [own, other], 1 << 33)
    for k in range(1, size // BLOCK):
        m = call(functools.partial(sweep_kernel, k), f32(size, size), [], [m], 1 << 33)
    return m


def first_join_kernel(flags, inv, own, other, mid, t_ref, kept):
    first = flags[1] == 0
    near = jnp.concatenate([pick(first, own[...], other[...]), pick(first, other[...], own[...])], axis=0)
    t = mm(inv[...], near)
    t_ref[...] = t
    rows = tmm(turned(flags[1] == 1, near)[:, : near.shape[1] // 2], turned(flags[1] == 1, t))
    kept[...] = mid[...] - cut(rows)


def edge_kernel(flags, inv, t, own, other, c_ref, c_half, base):
    core, side = flags[1], flags[3]
    first = core == 0
    width = t.shape[0]
    half = width // 2
    top = pick(first, own[...], other[...])
    low = pick(first, other[...], own[...])
    far = jnp.concatenate([top[:, :width], low[:, :width]], axis=0)
    c = -tmm(far, t[...])
    c_ref[...] = c
    c_half[...] = pick(first, c[:half], c[half:])
    here = pick(side == 0, top[:, width:], low[:, width:])
    there = pick(side == 0, low[:, width:], top[:, width:])
    edge = turned(side == 1, far)
    rows = full_rows(here, there) - mm(tmm(edge[:, :half], inv[...]), edge)
    base[...] = turned(side == 1, rows)


def last_join_kernel(flags, inv, c, own, other, base, o_ref):
    first, side, early = flags[1] == 0, flags[3], flags[4] == 0
    width = c.shape[0]
    half = width // 2
    z = mm(pick(side == 0, c[:half, :], c[half:, :]), inv[...])
    out_own = base[...] - nt(z, c[...])
    top = -nt(z, pick(first, own[...], other[...]))
    low = -nt(z, pick(first, other[...], own[...]))
    out_other = jnp.concatenate([top, low], axis=1)
    o_ref[:, :width] = pick(early, out_own, out_other)
    o_ref[:, width:] = pick(early, out_other, out_own)


def gram_kernel(flags, f_ref, o_ref):
    core, x_at = flags[1], flags[5]
    both = jnp.concatenate([f_ref[0].astype(jnp.bfloat16), f_ref[1].astype(jnp.bfloat16)], axis=1)
    pieces = []
    for z in range(8):
        here = pl.ds(pl.multiple_of(x_at * 512 + z * 64 + core * 32, 32), 32)
        pieces.append(jnp.concatenate([f_ref[0, here, :], f_ref[1, here, :]], axis=1).astype(jnp.bfloat16))
    lhs = jnp.concatenate(pieces, axis=0)
    total = lax.dot_general(lhs, both, (((1,), (1,)), ((), ())), preferred_element_type=jnp.float32)

    @pl.when(pl.program_id(0) == 0)
    def _():
        o_ref[...] = total

    @pl.when(pl.program_id(0) != 0)
    def _():
        o_ref[...] = o_ref[...] + total


def gram(flags, wide):
    count, nv, depth = wide.shape
    rows = nv // 8
    return pl.pallas_call(
        gram_kernel,
        grid=(count // 2,),
        out_shape=f32(rows, nv),
        in_specs=[SMEM_SPEC, pl.BlockSpec((2, nv, depth), lambda i: (i, 0, 0))],
        out_specs=pl.BlockSpec((rows, nv), lambda i: (0, 0)),
        compiler_params=pltpu.CompilerParams(vmem_limit_bytes=32 << 20),
        cost_estimate=pl.CostEstimate(
            flops=2 * count * rows * nv * depth, bytes_accessed=4 * count * nv * depth, transcendentals=0
        ),
    )(flags, wide)


def exchange(v, axes):
    return lax.all_to_all(v, axes, 0, 0, tiled=True)


def rows_sum(v):
    return jnp.sum(exchange(v.reshape(32, v.shape[0] // 32, v.shape[1]), ("x", "z")), axis=0)


def rows_gather(v):
    return exchange(jnp.broadcast_to(v[None], (32,) + v.shape), ("x", "z")).reshape(32 * v.shape[0], v.shape[1])


def tie(v, *others):
    return lax.optimization_barrier((v,) + others)[0]


def other_core(v):
    return lax.ppermute(v, "core", [(0, 1), (1, 0)])


def partner(v, mask):
    return lax.ppermute(v, "period", [(i, i ^ mask) for i in range(4)])


def on_device(factors, pattern, hessian, ramp_map):
    factor = factors[0, 0]
    nv, block_rows = factor.shape
    rows = hessian.shape[1]
    core = lax.axis_index("core")
    x_at = lax.axis_index("x")
    start = ((x_at * 8 + lax.axis_index("z")) * 2 + core) * rows
    period = lax.axis_index("period")
    middle_period = (period == 1) | (period == 2)
    flags = jnp.stack([period % 2, core, start, period % 2, period // 2, x_at]).astype(jnp.int32)

    with jax.named_scope("schur_gather"):
        present = jnp.repeat(pattern[0, 0], block_rows).astype(jnp.float32)
        wide = lax.optimization_barrier(factor.astype(jnp.float32) * present[:, None])
        wide = lax.all_gather(wide, ("x", "core"))

    with jax.named_scope("interface_partial"):
        mine, theirs = call(
            partial_kernel,
            [f32(256, 1280)] * 2,
            [flags, pattern[0, 0]],
            [factor, ramp_map[0], hessian[0][:, None]],
            1 << 30,
        )

    with jax.named_scope("interface_sum"):
        total = rows_sum(mine + other_core(theirs))
        beside = partner(total, 1)
        inner = rows_gather(total[:, :384] + beside[:, :384])
        near = jnp.where(middle_period, total[:, 384:], beside[:, 384:])
        far = jnp.where(middle_period, beside[:, 384:], total[:, 384:])
        inner_other = other_core(inner)
        near = rows_gather(tie(near, inner))
        near_other = other_core(near[:, :512])
        far = rows_gather(tie(far, near))
        far_other = other_core(far)

    with jax.named_scope("first_join"):
        inv1 = inverse(flags, inner, inner_other)
        t, kept = call(
            first_join_kernel,
            [f32(512, 512), f32(256, 384)],
            [flags],
            [inv1, near[:, :512], near_other, near[:, 512:]],
            1 << 32,
        )
        kept = kept + partner(kept, 3)
        kept_other = other_core(kept)
        c, c_half, base = call(
            edge_kernel, [f32(512, 512), f32(256, 512), f32(256, 512)], [flags], [inv1, t, far, far_other], 1 << 32
        )
        c_half = partner(tie(c_half, kept), 3)
        c_half_other = other_core(c_half)

    with jax.named_scope("schur_sum"):
        partial_sum = gram(flags, wide.reshape(8, nv, block_rows))
        schur_rows = lax.psum_scatter(partial_sum, "z", scatter_dimension=0, tiled=True)
        column_ids = lax.broadcasted_iota(jnp.int32, (rows, nv), 1)
        row_ids = lax.broadcasted_iota(jnp.int32, (rows, nv), 0) + start
        schur_rows = schur_rows + jnp.where(column_ids == row_ids, hessian[0][:, None], jnp.float32(0.0))

    with jax.named_scope("last_join"):
        inv2 = inverse(flags, kept, kept_other)
        my_rows = call(last_join_kernel, f32(256, 1024), [flags], [inv2, c, c_half, c_half_other, base], 1 << 31)
    return (schur_rows[None], my_rows)


def solution(mesh):
    fine = Mesh(mesh.devices.reshape(4, 4, 8, 2), ("period",) + CONT_AXES)
    in_specs = (
        P("period", CONT_AXES, None, None),
        P("period", CONT_AXES, None),
        P("period", CONT_AXES),
        P("period", None, None),
    )
    out_specs = (P("period", CONT_AXES, None), P("period", None))
    return jax.shard_map(on_device, mesh=fine, in_specs=in_specs, out_specs=out_specs, check_vma=False)
```

```python
import functools
import jax
import jax.numpy as jnp
from jax import lax
from jax.experimental import pallas as pl
from jax.experimental.pallas import tpu as pltpu
from jax.sharding import Mesh, PartitionSpec as P

HIGHEST = lax.Precision.HIGHEST
BLOCK = 128
PIVOT = 8
CONT_AXES = ("x", "z", "core")


def inverse_2(a, b, d):
    scale = 1.0 / (a * d - b * b)
    return d * scale, -b * scale, a * scale


def inverse_4(s):
    a, b, d = inverse_2(s[0][0], s[0][1], s[1][1])
    q = [[s[i][2], s[i][3]] for i in range(2)]
    t = [[a * q[0][j] + b * q[1][j] for j in range(2)], [b * q[0][j] + d * q[1][j] for j in range(2)]]
    e = s[2][2] - (q[0][0] * t[0][0] + q[1][0] * t[1][0])
    f = s[2][3] - (q[0][0] * t[0][1] + q[1][0] * t[1][1])
    g = s[3][3] - (q[0][1] * t[0][1] + q[1][1] * t[1][1])
    x, y, w = inverse_2(e, f, g)
    u = [[t[i][0] * x + t[i][1] * y, t[i][0] * y + t[i][1] * w] for i in range(2)]
    i00 = a + u[0][0] * t[0][0] + u[0][1] * t[0][1]
    i01 = b + u[0][0] * t[1][0] + u[0][1] * t[1][1]
    i11 = d + u[1][0] * t[1][0] + u[1][1] * t[1][1]
    n = [[-v for v in row] for row in u]
    return [[i00, i01] + n[0], [i01, i11] + n[1], [n[0][0], n[1][0], x, y], [n[0][1], n[1][1], y, w]]


def inverse_8(s):
    span = range(4)
    q = [row[4:] for row in s[:4]]
    corner = inverse_4([row[:4] for row in s[:4]])
    t = [[sum(corner[i][k] * q[k][j] for k in span) for j in span] for i in span]
    rest = [[None] * 4 for _ in span]
    for i in span:
        for j in range(i, 4):
            rest[i][j] = rest[j][i] = s[4 + i][4 + j] - sum(q[k][i] * t[k][j] for k in span)
    low = inverse_4(rest)
    u = [[sum(t[i][k] * low[k][j] for k in span) for j in span] for i in span]
    top = [[None] * 4 for _ in span]
    for i in span:
        for j in range(i, 4):
            top[i][j] = top[j][i] = corner[i][j] + sum(u[i][k] * t[j][k] for k in span)
    return [top[i] + [-v for v in u[i]] for i in span] + [[-u[j][i] for j in span] + low[i] for i in span]


def invert_block(a):
    lane = lax.broadcasted_iota(jnp.int32, (1, BLOCK), 1)
    sub = lax.broadcasted_iota(jnp.int32, (BLOCK, 1), 0)
    span = range(PIVOT)
    for k in range(0, BLOCK, PIVOT):
        rows = [a[k + i : k + i + 1, :] for i in span]
        cols = [a[:, k + i : k + i + 1] for i in span]
        s = [[None] * PIVOT for _ in span]
        for i in span:
            for j in range(i, PIVOT):
                s[i][j] = s[j][i] = jnp.broadcast_to(a[k + i : k + i + 1, k + j : k + j + 1], (1, BLOCK))
        s = inverse_8(s)
        lane_in = (lane >= k) & (lane < k + PIVOT)
        sub_in = (sub >= k) & (sub < k + PIVOT)
        ident = [jnp.where(lane == k + i, 1.0, jnp.where(lane_in, 0.0, rows[i])) for i in span]
        new_rows = [sum(s[i][j] * ident[j] for j in span) for i in span]
        a = jnp.where(lane_in | sub_in, 0.0, a)
        for i in span:
            a = a - jnp.where(sub == k + i, -1.0, jnp.where(sub_in, 0.0, cols[i])) * new_rows[i]
    return a


def mm(a, b):
    return jnp.dot(a, b, precision=HIGHEST, preferred_element_type=jnp.float32)


def tmm(a, b):
    dims = (((0,), (0,)), ((), ()))
    return lax.dot_general(a, b, dims, precision=HIGHEST, preferred_element_type=jnp.float32)


def nt(a, b):
    dims = (((1,), (1,)), ((), ()))
    return lax.dot_general(a, b, dims, precision=HIGHEST, preferred_element_type=jnp.float32)


def pick(first, a, b):
    return jnp.where(first, a, b)


def turned(second, a):
    half = a.shape[1] // 2
    return jnp.where(second, jnp.concatenate([a[:, half:], a[:, :half]], axis=1), a)


def cut(rows):
    return jnp.concatenate([rows[:BLOCK, : 3 * BLOCK], rows[BLOCK:, BLOCK:]], axis=0)


def tile(half, row, place):
    return half[row * BLOCK : (row + 1) * BLOCK, place * BLOCK : (place + 1) * BLOCK]


def full_rows(here, there):
    top = jnp.concatenate([here[:BLOCK], tile(there, 1, 1).T], axis=1)
    low = jnp.concatenate([tile(here, 0, 1).T, here[BLOCK:]], axis=1)
    return jnp.concatenate([top, low], axis=0)


VMEM_SPEC = pl.BlockSpec(memory_space=pltpu.VMEM)
SMEM_SPEC = pl.BlockSpec(memory_space=pltpu.SMEM)


def f32(*shape):
    return jax.ShapeDtypeStruct(shape, jnp.float32)


def call(kernel, out_shape, scalars, arrays, flops):
    many = isinstance(out_shape, (list, tuple))
    moved = sum(a.size * a.dtype.itemsize for a in arrays)
    return pl.pallas_call(
        kernel,
        out_shape=out_shape,
        in_specs=[SMEM_SPEC] * len(scalars) + [VMEM_SPEC] * len(arrays),
        out_specs=[VMEM_SPEC] * len(out_shape) if many else VMEM_SPEC,
        compiler_params=pltpu.CompilerParams(vmem_limit_bytes=16 << 20),
        cost_estimate=pl.CostEstimate(flops=flops, bytes_accessed=moved, transcendentals=0),
    )(*scalars, *arrays)


def partial_kernel(flags, pattern, factor, ramp, hess, mine, theirs):
    even, core = flags[0] == 0, flags[1]
    start = pl.multiple_of(flags[2], 32)
    half = ramp.shape[1] // 2
    blocks = pattern.shape[0]
    masked = jnp.concatenate(
        [
            jnp.where(pattern[b] != 0, factor[b * BLOCK : (b + 1) * BLOCK, :], jnp.bfloat16(0))
            for b in range(blocks)
        ],
        axis=0,
    )
    image = lax.dot_general(masked, ramp[...], (((0,), (0,)), ((), ())), preferred_element_type=jnp.float32)
    ramp_rows = ramp[pl.ds(start, 32), :].astype(jnp.float32)
    left = jnp.concatenate([image, ramp_rows * hess[...]], axis=0)
    right = jnp.concatenate([image, ramp_rows], axis=0)
    inner_left = pick(even, left[:, half:], left[:, :half])
    inner_right = pick(even, right[:, half:], right[:, :half])
    outer_left = pick(even, left[:, :half], left[:, half:])
    outer_right = pick(even, right[:, :half], right[:, half:])
    for out, q in ((mine, core), (theirs, 1 - core)):
        inner_half = turned(q == 1, inner_left)[:, : half // 2]
        outer_half = turned(q == 1, outer_left)[:, : half // 2]
        out[:, :384] = cut(tmm(inner_half, turned(q == 1, inner_right)))
        out[:, 384:896] = tmm(inner_half, outer_right)
        out[:, 896:] = cut(tmm(outer_half, turned(q == 1, outer_right)))


def sweep(k, source, ref):
    size = source.shape[0]
    off = k * BLOCK
    end = off + BLOCK
    inv = invert_block(source[off:end, off:end])
    pieces = [inv]
    if off > 0:
        pieces = [mm(inv, source[off:end, :off])] + pieces
    if end < size:
        pieces = pieces + [mm(inv, source[off:end, end:])]
    rows = jnp.concatenate(pieces, axis=1)
    col_id = lax.broadcasted_iota(jnp.int32, (1, size), 1)
    col_in = (col_id >= off) & (col_id < end)
    for low in range(0, size, BLOCK):
        if low != off:
            here = source[low : low + BLOCK, :]
            ref[low : low + BLOCK, :] = jnp.where(col_in, 0.0, here) - mm(here[:, off:end], rows)
    ref[off:end, :] = rows


def first_sweep_kernel(flags, own, other, o_ref):
    first = flags[1] == 0
    top = pick(first, own[:, :384], other[:, :384])
    low = pick(first, other[:, :384], own[:, :384])
    half = top.shape[0]
    o_ref[:half, :] = full_rows(top, low)
    low_rows = full_rows(low, top)
    o_ref[half:, :half] = low_rows[:, half:]
    o_ref[half:, half:] = low_rows[:, :half]
    sweep(0, o_ref, o_ref)


def inverse(flags, own, other):
    size = 2 * own.shape[0]
    m = call(first_sweep_kernel, f32(size, size), [flags], [own, other], 1 << 33)
    for k in range(1, size // BLOCK):
        m = call(functools.partial(sweep, k), f32(size, size), [], [m], 1 << 33)
    return m


def first_join_kernel(flags, inv, own, other, t_ref, kept):
    first = flags[1] == 0
    mine, theirs = own[:, 384:896], other[:, 384:896]
    near = jnp.concatenate([pick(first, mine, theirs), pick(first, theirs, mine)], axis=0)
    t = mm(inv[...], near)
    t_ref[...] = t
    rows = tmm(turned(flags[1] == 1, near)[:, : near.shape[1] // 2], turned(flags[1] == 1, t))
    kept[...] = own[:, 896:] - cut(rows)


def edge_kernel(flags, inv, t, own, other, c_ref, c_half, base):
    core, side = flags[1], flags[3]
    first = core == 0
    width = t.shape[0]
    half = width // 2
    top = pick(first, own[...], other[...])
    low = pick(first, other[...], own[...])
    far = jnp.concatenate([top[:, :width], low[:, :width]], axis=0)
    c = -tmm(far, t[...])
    c_ref[...] = c
    c_half[...] = pick(first, c[:half], c[half:])
    here = pick(side == 0, top[:, width:], low[:, width:])
    there = pick(side == 0, low[:, width:], top[:, width:])
    edge = turned(side == 1, far)
    rows = full_rows(here, there) - mm(tmm(edge[:, :half], inv[...]), edge)
    base[...] = turned(side == 1, rows)


def last_join_kernel(flags, inv, c, own, other, base, o_ref):
    first, side, early = flags[1] == 0, flags[3], flags[4] == 0
    width = c.shape[0]
    half = width // 2
    z = mm(pick(side == 0, c[:half, :], c[half:, :]), inv[...])
    out_own = base[...] - nt(z, c[...])
    top = -nt(z, pick(first, own[...], other[...]))
    low = -nt(z, pick(first, other[...], own[...]))
    out_other = jnp.concatenate([top, low], axis=1)
    o_ref[:, :width] = pick(early, out_own, out_other)
    o_ref[:, width:] = pick(early, out_other, out_own)


def gram_kernel(flags, f_ref, hess, o_ref):
    core, x_at = flags[1], flags[5]
    both = jnp.concatenate([f_ref[0].astype(jnp.bfloat16), f_ref[1].astype(jnp.bfloat16)], axis=1)
    pieces = []
    for z in range(8):
        here = pl.ds(pl.multiple_of(x_at * 512 + z * 64 + core * 32, 32), 32)
        pieces.append(jnp.concatenate([f_ref[0, here, :], f_ref[1, here, :]], axis=1).astype(jnp.bfloat16))
    lhs = jnp.concatenate(pieces, axis=0)
    total = lax.dot_general(lhs, both, (((1,), (1,)), ((), ())), preferred_element_type=jnp.float32)

    @pl.when(pl.program_id(0) == 0)
    def _():
        o_ref[...] = total

    @pl.when(pl.program_id(0) != 0)
    def _():
        o_ref[...] = o_ref[...] + total

    @pl.when(pl.program_id(0) == pl.num_programs(0) - 1)
    def _():
        own = pl.ds(pl.multiple_of(flags[6] * 32, 32), 32)
        shape = (32, o_ref.shape[1])
        on_diag = lax.broadcasted_iota(jnp.int32, shape, 1) == lax.broadcasted_iota(jnp.int32, shape, 0) + flags[2]
        o_ref[own, :] = o_ref[own, :] + jnp.where(on_diag, hess[...], 0.0)


def gram(flags, wide, hess):
    count, nv, depth = wide.shape
    rows = nv // 8
    return pl.pallas_call(
        gram_kernel,
        grid=(count // 2,),
        out_shape=f32(rows, nv),
        in_specs=[
            SMEM_SPEC,
            pl.BlockSpec((2, nv, depth), lambda i: (i, 0, 0)),
            pl.BlockSpec(hess.shape, lambda i: (0, 0)),
        ],
        out_specs=pl.BlockSpec((rows, nv), lambda i: (0, 0)),
        compiler_params=pltpu.CompilerParams(vmem_limit_bytes=16 << 20),
        cost_estimate=pl.CostEstimate(
            flops=2 * count * rows * nv * depth, bytes_accessed=4 * count * nv * depth, transcendentals=0
        ),
    )(flags, wide, hess)


def exchange(v, axes):
    return lax.all_to_all(v, axes, 0, 0, tiled=True)


def rows_sum(v):
    return jnp.sum(exchange(v.reshape(32, v.shape[0] // 32, v.shape[1]), ("x", "z")), axis=0)


def rows_gather(v):
    return exchange(jnp.broadcast_to(v[None], (32,) + v.shape), ("x", "z")).reshape(32 * v.shape[0], v.shape[1])


def tie(v, *others):
    return lax.optimization_barrier((v,) + others)[0]


def other_core(v):
    return lax.ppermute(v, "core", [(0, 1), (1, 0)])


def partner(v, mask):
    return lax.ppermute(v, "period", [(i, i ^ mask) for i in range(4)])


def on_device(factors, pattern, hessian, ramp_map):
    factor = factors[0, 0]
    nv, block_rows = factor.shape
    rows = hessian.shape[1]
    core = lax.axis_index("core")
    x_at = lax.axis_index("x")
    z_at = lax.axis_index("z")
    start = ((x_at * 8 + z_at) * 2 + core) * rows
    period = lax.axis_index("period")
    middle_period = (period == 1) | (period == 2)
    flags = jnp.stack([period % 2, core, start, period % 2, period // 2, x_at, z_at]).astype(jnp.int32)

    hess = hessian[0][:, None]

    with jax.named_scope("interface_partial"):
        mine, theirs = call(
            partial_kernel,
            [f32(256, 1280)] * 2,
            [flags, pattern[0, 0]],
            [factor, ramp_map[0], hess],
            1 << 30,
        )

    with jax.named_scope("interface_sum"):
        total = rows_sum(mine + other_core(theirs))

    with jax.named_scope("schur_gather"):
        present = jnp.repeat(pattern[0, 0], block_rows).astype(jnp.float32)
        wide = lax.optimization_barrier(factor.astype(jnp.float32) * present[:, None])
        wide = lax.all_gather(tie(wide, total), ("x", "core"))

    with jax.named_scope("interface_gather"):
        beside = partner(total, 1)
        near = jnp.where(middle_period, total[:, 384:], beside[:, 384:])
        far = jnp.where(middle_period, beside[:, 384:], total[:, 384:])
        first = rows_gather(jnp.concatenate([total[:, :384] + beside[:, :384], near], axis=1))
        first_other = other_core(first)
        far = rows_gather(tie(far, first))

    with jax.named_scope("first_join"):
        inv1 = inverse(flags, first, first_other)
        t, kept = call(
            first_join_kernel, [f32(512, 512), f32(256, 384)], [flags], [inv1, first, first_other], 1 << 32
        )
        partial_sum = gram(flags, tie(wide, kept).reshape(8, nv, block_rows), hess)
        kept = kept + tie(partner(kept, 3), partial_sum)
        far = tie(far, kept)
        far_other = other_core(far)
        kept_other = other_core(kept)
        c, c_half, base = call(
            edge_kernel, [f32(512, 512), f32(256, 512), f32(256, 512)], [flags], [inv1, t, far, far_other], 1 << 32
        )
        c_half = partner(tie(c_half, kept), 3)
        c_half_other = other_core(c_half)

    with jax.named_scope("schur_sum"):
        schur_rows = lax.psum_scatter(partial_sum, "z", scatter_dimension=0, tiled=True)

    with jax.named_scope("last_join"):
        inv2 = inverse(flags, kept, tie(kept_other, base))
        my_rows = call(last_join_kernel, f32(256, 1024), [flags], [inv2, c, c_half, c_half_other, base], 1 << 31)
    return (schur_rows[None], my_rows)


def solution(mesh):
    fine = Mesh(mesh.devices.reshape(4, 4, 8, 2), ("period",) + CONT_AXES)
    in_specs = (
        P("period", CONT_AXES, None, None),
        P("period", CONT_AXES, None),
        P("period", CONT_AXES),
        P("period", None, None),
    )
    out_specs = (P("period", CONT_AXES, None), P("period", None))
    return jax.shard_map(on_device, mesh=fine, in_specs=in_specs, out_specs=out_specs, check_vma=False)
```

```python
import functools
import jax
import jax.numpy as jnp
from jax import lax
from jax.experimental import pallas as pl
from jax.experimental.pallas import tpu as pltpu
from jax.sharding import Mesh, PartitionSpec as P

HIGHEST = lax.Precision.HIGHEST
BLOCK = 128
PIVOT = 8
CONT_AXES = ("x", "z", "core")


def inverse_2(a, b, d):
    scale = 1.0 / (a * d - b * b)
    return d * scale, -b * scale, a * scale


def inverse_4(s):
    a, b, d = inverse_2(s[0][0], s[0][1], s[1][1])
    q = [[s[i][2], s[i][3]] for i in range(2)]
    t = [[a * q[0][j] + b * q[1][j] for j in range(2)], [b * q[0][j] + d * q[1][j] for j in range(2)]]
    e = s[2][2] - (q[0][0] * t[0][0] + q[1][0] * t[1][0])
    f = s[2][3] - (q[0][0] * t[0][1] + q[1][0] * t[1][1])
    g = s[3][3] - (q[0][1] * t[0][1] + q[1][1] * t[1][1])
    x, y, w = inverse_2(e, f, g)
    u = [[t[i][0] * x + t[i][1] * y, t[i][0] * y + t[i][1] * w] for i in range(2)]
    i00 = a + u[0][0] * t[0][0] + u[0][1] * t[0][1]
    i01 = b + u[0][0] * t[1][0] + u[0][1] * t[1][1]
    i11 = d + u[1][0] * t[1][0] + u[1][1] * t[1][1]
    n = [[-v for v in row] for row in u]
    return [[i00, i01] + n[0], [i01, i11] + n[1], [n[0][0], n[1][0], x, y], [n[0][1], n[1][1], y, w]]


def inverse_8(s):
    span = range(4)
    q = [row[4:] for row in s[:4]]
    corner = inverse_4([row[:4] for row in s[:4]])
    t = [[sum(corner[i][k] * q[k][j] for k in span) for j in span] for i in span]
    rest = [[None] * 4 for _ in span]
    for i in span:
        for j in range(i, 4):
            rest[i][j] = rest[j][i] = s[4 + i][4 + j] - sum(q[k][i] * t[k][j] for k in span)
    low = inverse_4(rest)
    u = [[sum(t[i][k] * low[k][j] for k in span) for j in span] for i in span]
    top = [[None] * 4 for _ in span]
    for i in span:
        for j in range(i, 4):
            top[i][j] = top[j][i] = corner[i][j] + sum(u[i][k] * t[j][k] for k in span)
    return [top[i] + [-v for v in u[i]] for i in span] + [[-u[j][i] for j in span] + low[i] for i in span]


def invert_block(a):
    lane = lax.broadcasted_iota(jnp.int32, (1, BLOCK), 1)
    sub = lax.broadcasted_iota(jnp.int32, (BLOCK, 1), 0)
    span = range(PIVOT)
    for k in range(0, BLOCK, PIVOT):
        rows = [a[k + i : k + i + 1, :] for i in span]
        cols = [a[:, k + i : k + i + 1] for i in span]
        s = [[None] * PIVOT for _ in span]
        for i in span:
            for j in range(i, PIVOT):
                s[i][j] = s[j][i] = jnp.broadcast_to(a[k + i : k + i + 1, k + j : k + j + 1], (1, BLOCK))
        s = inverse_8(s)
        lane_in = (lane >= k) & (lane < k + PIVOT)
        sub_in = (sub >= k) & (sub < k + PIVOT)
        ident = [jnp.where(lane == k + i, 1.0, jnp.where(lane_in, 0.0, rows[i])) for i in span]
        new_rows = [sum(s[i][j] * ident[j] for j in span) for i in span]
        a = jnp.where(lane_in | sub_in, 0.0, a)
        for i in span:
            a = a - jnp.where(sub == k + i, -1.0, jnp.where(sub_in, 0.0, cols[i])) * new_rows[i]
    return a


def mm(a, b):
    return jnp.dot(a, b, precision=HIGHEST, preferred_element_type=jnp.float32)


def tmm(a, b):
    dims = (((0,), (0,)), ((), ()))
    return lax.dot_general(a, b, dims, precision=HIGHEST, preferred_element_type=jnp.float32)


def nt(a, b):
    dims = (((1,), (1,)), ((), ()))
    return lax.dot_general(a, b, dims, precision=HIGHEST, preferred_element_type=jnp.float32)


def pick(first, a, b):
    return jnp.where(first, a, b)


def turned(second, a):
    half = a.shape[1] // 2
    return jnp.where(second, jnp.concatenate([a[:, half:], a[:, :half]], axis=1), a)


def cut(rows):
    return jnp.concatenate([rows[:BLOCK, : 3 * BLOCK], rows[BLOCK:, BLOCK:]], axis=0)


def tile(half, row, place):
    return half[row * BLOCK : (row + 1) * BLOCK, place * BLOCK : (place + 1) * BLOCK]


def full_rows(here, there):
    top = jnp.concatenate([here[:BLOCK], tile(there, 1, 1).T], axis=1)
    low = jnp.concatenate([tile(here, 0, 1).T, here[BLOCK:]], axis=1)
    return jnp.concatenate([top, low], axis=0)


VMEM_SPEC = pl.BlockSpec(memory_space=pltpu.VMEM)
SMEM_SPEC = pl.BlockSpec(memory_space=pltpu.SMEM)


def f32(*shape):
    return jax.ShapeDtypeStruct(shape, jnp.float32)


def call(kernel, out_shape, scalars, arrays, flops):
    many = isinstance(out_shape, (list, tuple))
    moved = sum(a.size * a.dtype.itemsize for a in arrays)
    return pl.pallas_call(
        kernel,
        out_shape=out_shape,
        in_specs=[SMEM_SPEC] * len(scalars) + [VMEM_SPEC] * len(arrays),
        out_specs=[VMEM_SPEC] * len(out_shape) if many else VMEM_SPEC,
        compiler_params=pltpu.CompilerParams(vmem_limit_bytes=16 << 20),
        cost_estimate=pl.CostEstimate(flops=flops, bytes_accessed=moved, transcendentals=0),
    )(*scalars, *arrays)


def as_column(row):
    n = row.shape[1]
    eye = lax.broadcasted_iota(jnp.int32, (n, n), 0) == lax.broadcasted_iota(jnp.int32, (n, n), 1)
    return jnp.sum(jnp.where(eye, row, 0.0), axis=1, keepdims=True)


def partial_kernel(flags, pattern, factor, ramp, hess, mine, theirs, image, ramp_rows):
    step = pl.program_id(0)
    chunk = ramp.shape[1]
    blocks = chunk // BLOCK
    masked = jnp.concatenate(
        [
            jnp.where(
                pattern[0, 0, step * blocks + b] != 0,
                factor[0, 0, b * BLOCK : (b + 1) * BLOCK, :],
                jnp.bfloat16(0),
            )
            for b in range(blocks)
        ],
        axis=0,
    )
    here = lax.dot_general(masked, ramp[0], (((0,), (0,)), ((), ())), preferred_element_type=jnp.float32)

    @pl.when(step == 0)
    def _():
        image[...] = here

    @pl.when(step != 0)
    def _():
        image[...] = image[...] + here

    @pl.when(flags[2] // chunk == step)
    def _():
        start = pl.multiple_of(flags[2] - step * chunk, 32)
        ramp_rows[...] = ramp[0, pl.ds(start, 32), :].astype(jnp.float32)

    @pl.when(step == pl.num_programs(0) - 1)
    def _():
        even, core = flags[0] == 0, flags[1]
        half = image.shape[1] // 2
        left = jnp.concatenate([image[...], ramp_rows[...] * as_column(hess[...])], axis=0)
        right = jnp.concatenate([image[...], ramp_rows[...]], axis=0)
        inner_left = pick(even, left[:, half:], left[:, :half])
        inner_right = pick(even, right[:, half:], right[:, :half])
        outer_left = pick(even, left[:, :half], left[:, half:])
        outer_right = pick(even, right[:, :half], right[:, half:])
        for out, q in ((mine, core), (theirs, 1 - core)):
            inner_half = turned(q == 1, inner_left)[:, : half // 2]
            outer_half = turned(q == 1, outer_left)[:, : half // 2]
            out[:, :384] = cut(tmm(inner_half, turned(q == 1, inner_right)))
            out[:, 384:896] = tmm(inner_half, outer_right)
            out[:, 896:] = cut(tmm(outer_half, turned(q == 1, outer_right)))


def partial(flags, pattern, factors, ramp_map, hess):
    _, _, nv, depth = factors.shape
    iface = ramp_map.shape[2]
    chunk = nv // 4
    return pl.pallas_call(
        partial_kernel,
        grid=(nv // chunk,),
        out_shape=[f32(256, 1280)] * 2,
        in_specs=[
            SMEM_SPEC,
            SMEM_SPEC,
            pl.BlockSpec((1, 1, chunk, depth), lambda i: (0, 0, i, 0)),
            pl.BlockSpec((1, chunk, iface), lambda i: (0, i, 0)),
            pl.BlockSpec(hess.shape, lambda i: (0, 0)),
        ],
        out_specs=[pl.BlockSpec((256, 1280), lambda i: (0, 0))] * 2,
        scratch_shapes=[pltpu.VMEM((depth, iface), jnp.float32), pltpu.VMEM((32, iface), jnp.float32)],
        compiler_params=pltpu.CompilerParams(vmem_limit_bytes=60 << 20),
        cost_estimate=pl.CostEstimate(flops=1 << 30, bytes_accessed=5 << 20, transcendentals=0),
    )(flags, pattern, factors, ramp_map, hess)


def sweep(k, source, ref):
    size = source.shape[0]
    off = k * BLOCK
    end = off + BLOCK
    inv = invert_block(source[off:end, off:end])
    pieces = [inv]
    if off > 0:
        pieces = [mm(inv, source[off:end, :off])] + pieces
    if end < size:
        pieces = pieces + [mm(inv, source[off:end, end:])]
    rows = jnp.concatenate(pieces, axis=1)
    col_id = lax.broadcasted_iota(jnp.int32, (1, size), 1)
    col_in = (col_id >= off) & (col_id < end)
    for low in range(0, size, BLOCK):
        if low != off:
            here = source[low : low + BLOCK, :]
            ref[low : low + BLOCK, :] = jnp.where(col_in, 0.0, here) - mm(here[:, off:end], rows)
    ref[off:end, :] = rows


def first_sweep_kernel(flags, own, other, o_ref):
    first = flags[1] == 0
    top = pick(first, own[:, :384], other[:, :384])
    low = pick(first, other[:, :384], own[:, :384])
    half = top.shape[0]
    o_ref[:half, :] = full_rows(top, low)
    low_rows = full_rows(low, top)
    o_ref[half:, :half] = low_rows[:, half:]
    o_ref[half:, half:] = low_rows[:, :half]
    sweep(0, o_ref, o_ref)


def later_sweep(k, flags, source, ref):
    sweep(k, source, ref)


def inverse(flags, own, other, hook=None):
    size = 2 * own.shape[0]
    m = call(first_sweep_kernel, f32(size, size), [flags], [own, other], 1 << 33)
    if hook is not None:
        flags = tie(flags, hook)
    for k in range(1, size // BLOCK):
        m = call(functools.partial(later_sweep, k), f32(size, size), [flags], [m], 1 << 33)
    return m


def first_join_kernel(flags, inv, own, other, t_ref, removed):
    first = flags[1] == 0
    mine, theirs = own[:, 384:896], other[:, 384:896]
    near = jnp.concatenate([pick(first, mine, theirs), pick(first, theirs, mine)], axis=0)
    t = mm(inv[...], near)
    t_ref[...] = t
    rows = tmm(turned(flags[1] == 1, near)[:, : near.shape[1] // 2], turned(flags[1] == 1, t))
    removed[...] = cut(rows)


def edge_kernel(flags, inv, t, own, other, c_ref, c_half, base):
    core, side = flags[1], flags[3]
    first = core == 0
    width = t.shape[0]
    half = width // 2
    top = pick(first, own[...], other[...])
    low = pick(first, other[...], own[...])
    far = jnp.concatenate([top[:, :width], low[:, :width]], axis=0)
    c = -tmm(far, t[...])
    c_ref[...] = c
    c_half[...] = pick(first, c[:half], c[half:])
    here = pick(side == 0, top[:, width:896], low[:, width:896])
    there = pick(side == 0, low[:, width:896], top[:, width:896])
    edge = turned(side == 1, far)
    rows = full_rows(here, there) - mm(tmm(edge[:, :half], inv[...]), edge)
    base[...] = turned(side == 1, rows)


def last_join_kernel(flags, inv, c, own, other, base, o_ref):
    first, side, early = flags[1] == 0, flags[3], flags[4] == 0
    width = c.shape[0]
    half = width // 2
    z = mm(pick(side == 0, c[:half, :], c[half:, :]), inv[...])
    out_own = base[...] - nt(z, c[...])
    top = -nt(z, pick(first, own[...], other[...]))
    low = -nt(z, pick(first, other[...], own[...]))
    out_other = jnp.concatenate([top, low], axis=1)
    o_ref[:, :width] = pick(early, out_own, out_other)
    o_ref[:, width:] = pick(early, out_other, out_own)


def gram_kernel(flags, f_ref, hess, o_ref):
    core, x_at = flags[1], flags[5]
    both = jnp.concatenate([f_ref[0].astype(jnp.bfloat16), f_ref[1].astype(jnp.bfloat16)], axis=1)
    pieces = []
    for z in range(8):
        here = pl.ds(pl.multiple_of(x_at * 512 + z * 64 + core * 32, 32), 32)
        pieces.append(jnp.concatenate([f_ref[0, here, :], f_ref[1, here, :]], axis=1).astype(jnp.bfloat16))
    lhs = jnp.concatenate(pieces, axis=0)
    total = lax.dot_general(lhs, both, (((1,), (1,)), ((), ())), preferred_element_type=jnp.float32)

    @pl.when(pl.program_id(0) == 0)
    def _():
        o_ref[...] = total

    @pl.when(pl.program_id(0) != 0)
    def _():
        o_ref[...] = o_ref[...] + total

    @pl.when(pl.program_id(0) == pl.num_programs(0) - 1)
    def _():
        own = pl.ds(pl.multiple_of(flags[6] * 32, 32), 32)
        shape = (32, o_ref.shape[1])
        on_diag = lax.broadcasted_iota(jnp.int32, shape, 1) == lax.broadcasted_iota(jnp.int32, shape, 0) + flags[2]
        o_ref[own, :] = o_ref[own, :] + jnp.where(on_diag, as_column(hess[...]), 0.0)


def gram(flags, wide, hess):
    count, nv, depth = wide.shape
    rows = nv // 8
    return pl.pallas_call(
        gram_kernel,
        grid=(count // 2,),
        out_shape=f32(rows, nv),
        in_specs=[
            SMEM_SPEC,
            pl.BlockSpec((2, nv, depth), lambda i: (i, 0, 0)),
            pl.BlockSpec(hess.shape, lambda i: (0, 0)),
        ],
        out_specs=pl.BlockSpec((rows, nv), lambda i: (0, 0)),
        compiler_params=pltpu.CompilerParams(vmem_limit_bytes=16 << 20),
        cost_estimate=pl.CostEstimate(
            flops=2 * count * rows * nv * depth, bytes_accessed=4 * count * nv * depth, transcendentals=0
        ),
    )(flags, wide, hess)


def exchange(v, axes):
    return lax.all_to_all(v, axes, 0, 0, tiled=True)


def rows_sum(v):
    return jnp.sum(exchange(v.reshape(32, v.shape[0] // 32, v.shape[1]), ("x", "z")), axis=0)


def rows_gather(v):
    return exchange(jnp.broadcast_to(v[None], (32,) + v.shape), ("x", "z")).reshape(32 * v.shape[0], v.shape[1])


def tie(v, *others):
    return lax.optimization_barrier((v,) + others)[0]


def other_core(v):
    return lax.ppermute(v, "core", [(0, 1), (1, 0)])


def partner(v, mask):
    return lax.ppermute(v, "period", [(i, i ^ mask) for i in range(4)])


def on_device(factors, pattern, hessian, ramp_map):
    factor = factors[0, 0]
    nv, block_rows = factor.shape
    rows = hessian.shape[1]
    core = lax.axis_index("core")
    x_at = lax.axis_index("x")
    z_at = lax.axis_index("z")
    start = ((x_at * 8 + z_at) * 2 + core) * rows
    period = lax.axis_index("period")
    middle_period = (period == 1) | (period == 2)
    flags = jnp.stack([period % 2, core, start, period % 2, period // 2, x_at, z_at]).astype(jnp.int32)

    with jax.named_scope("schur_gather"):
        present = jnp.repeat(pattern[0, 0], block_rows).astype(jnp.float32)
        wide = lax.optimization_barrier(factor.astype(jnp.float32) * present[:, None])

    with jax.named_scope("interface_partial"):
        mine, theirs = partial(flags, pattern, factors, ramp_map, hessian)

    with jax.named_scope("schur_gather"):
        wide = lax.all_gather(tie(wide, mine), ("x", "core"))

    with jax.named_scope("interface_sum"):
        total = rows_sum(mine + other_core(theirs))

    with jax.named_scope("schur_sum"):
        partial_sum = gram(flags, tie(wide, total).reshape(8, nv, block_rows), hessian)
        schur_rows = lax.psum_scatter(partial_sum, "z", scatter_dimension=0, tiled=True)

    with jax.named_scope("interface_gather"):
        beside = partner(total, 1)
        near = jnp.where(middle_period, total[:, 384:896], beside[:, 384:896])
        first = rows_gather(jnp.concatenate([total[:, :384] + beside[:, :384], near], axis=1))
        far = jnp.where(middle_period, beside[:, 384:], total[:, 384:])
        kept_outer = jnp.where(middle_period, total[:, 896:], beside[:, 896:])
        kept_outer = kept_outer + partner(kept_outer, 3)
        first = tie(first, partial_sum, kept_outer)
        first_other = other_core(first)
        far = rows_gather(tie(jnp.concatenate([far, kept_outer], axis=1), first))

    with jax.named_scope("first_join"):
        inv1 = inverse(flags, first, first_other)
        t, removed = call(
            first_join_kernel, [f32(512, 512), f32(256, 384)], [flags], [inv1, first, first_other], 1 << 32
        )
        removed = removed + partner(removed, 3)
        far = tie(far, removed)
        far_other = other_core(far)
        kept = far[:, 896:] - removed
        kept_other = other_core(kept)
        c, c_half, base = call(
            edge_kernel, [f32(512, 512), f32(256, 512), f32(256, 512)], [flags], [inv1, t, far, far_other], 1 << 32
        )
        c_half = partner(c_half, 3)
        c_half_other = other_core(c_half)

    with jax.named_scope("last_join"):
        inv2 = inverse(tie(flags, base), kept, kept_other, schur_rows)
        my_rows = call(last_join_kernel, f32(256, 1024), [flags], [inv2, c, c_half, c_half_other, base], 1 << 31)
    return (schur_rows[None], my_rows)


def solution(mesh):
    fine = Mesh(mesh.devices.reshape(4, 4, 8, 2), ("period",) + CONT_AXES)
    in_specs = (
        P("period", CONT_AXES, None, None),
        P("period", CONT_AXES, None),
        P("period", CONT_AXES),
        P("period", None, None),
    )
    out_specs = (P("period", CONT_AXES, None), P("period", None))
    return jax.shard_map(on_device, mesh=fine, in_specs=in_specs, out_specs=out_specs, check_vma=False)
```

```python
import functools
import jax
import jax.numpy as jnp
from jax import lax
from jax.experimental import pallas as pl
from jax.experimental.pallas import tpu as pltpu
from jax.sharding import Mesh, PartitionSpec as P

HIGHEST = lax.Precision.HIGHEST
BLOCK = 128
PIVOT = 8
CONT_AXES = ("x", "z", "core")


def inverse_2(a, b, d):
    scale = 1.0 / (a * d - b * b)
    return d * scale, -b * scale, a * scale


def inverse_4(s):
    a, b, d = inverse_2(s[0][0], s[0][1], s[1][1])
    q = [[s[i][2], s[i][3]] for i in range(2)]
    t = [[a * q[0][j] + b * q[1][j] for j in range(2)], [b * q[0][j] + d * q[1][j] for j in range(2)]]
    e = s[2][2] - (q[0][0] * t[0][0] + q[1][0] * t[1][0])
    f = s[2][3] - (q[0][0] * t[0][1] + q[1][0] * t[1][1])
    g = s[3][3] - (q[0][1] * t[0][1] + q[1][1] * t[1][1])
    x, y, w = inverse_2(e, f, g)
    u = [[t[i][0] * x + t[i][1] * y, t[i][0] * y + t[i][1] * w] for i in range(2)]
    i00 = a + u[0][0] * t[0][0] + u[0][1] * t[0][1]
    i01 = b + u[0][0] * t[1][0] + u[0][1] * t[1][1]
    i11 = d + u[1][0] * t[1][0] + u[1][1] * t[1][1]
    n = [[-v for v in row] for row in u]
    return [[i00, i01] + n[0], [i01, i11] + n[1], [n[0][0], n[1][0], x, y], [n[0][1], n[1][1], y, w]]


def inverse_8(s):
    span = range(4)
    q = [row[4:] for row in s[:4]]
    corner = inverse_4([row[:4] for row in s[:4]])
    t = [[sum(corner[i][k] * q[k][j] for k in span) for j in span] for i in span]
    rest = [[None] * 4 for _ in span]
    for i in span:
        for j in range(i, 4):
            rest[i][j] = rest[j][i] = s[4 + i][4 + j] - sum(q[k][i] * t[k][j] for k in span)
    low = inverse_4(rest)
    u = [[sum(t[i][k] * low[k][j] for k in span) for j in span] for i in span]
    top = [[None] * 4 for _ in span]
    for i in span:
        for j in range(i, 4):
            top[i][j] = top[j][i] = corner[i][j] + sum(u[i][k] * t[j][k] for k in span)
    return [top[i] + [-v for v in u[i]] for i in span] + [[-u[j][i] for j in span] + low[i] for i in span]


def invert_block(a):
    lane = lax.broadcasted_iota(jnp.int32, (1, BLOCK), 1)
    sub = lax.broadcasted_iota(jnp.int32, (BLOCK, 1), 0)
    span = range(PIVOT)
    for k in range(0, BLOCK, PIVOT):
        rows = [a[k + i : k + i + 1, :] for i in span]
        cols = [a[:, k + i : k + i + 1] for i in span]
        s = [[None] * PIVOT for _ in span]
        for i in span:
            for j in range(i, PIVOT):
                s[i][j] = s[j][i] = jnp.broadcast_to(a[k + i : k + i + 1, k + j : k + j + 1], (1, BLOCK))
        s = inverse_8(s)
        lane_in = (lane >= k) & (lane < k + PIVOT)
        sub_in = (sub >= k) & (sub < k + PIVOT)
        ident = [jnp.where(lane == k + i, 1.0, jnp.where(lane_in, 0.0, rows[i])) for i in span]
        new_rows = [sum(s[i][j] * ident[j] for j in span) for i in span]
        a = jnp.where(lane_in | sub_in, 0.0, a)
        for i in span:
            a = a - jnp.where(sub == k + i, -1.0, jnp.where(sub_in, 0.0, cols[i])) * new_rows[i]
    return a


def mm(a, b):
    return jnp.dot(a, b, precision=HIGHEST, preferred_element_type=jnp.float32)


def tmm(a, b):
    dims = (((0,), (0,)), ((), ()))
    return lax.dot_general(a, b, dims, precision=HIGHEST, preferred_element_type=jnp.float32)


def nt(a, b):
    dims = (((1,), (1,)), ((), ()))
    return lax.dot_general(a, b, dims, precision=HIGHEST, preferred_element_type=jnp.float32)


def pick(first, a, b):
    return jnp.where(first, a, b)


def turned(second, a):
    half = a.shape[1] // 2
    return jnp.where(second, jnp.concatenate([a[:, half:], a[:, :half]], axis=1), a)


def cut(rows):
    return jnp.concatenate([rows[:BLOCK, : 3 * BLOCK], rows[BLOCK:, BLOCK:]], axis=0)


def tile(half, row, place):
    return half[row * BLOCK : (row + 1) * BLOCK, place * BLOCK : (place + 1) * BLOCK]


def full_rows(here, there):
    top = jnp.concatenate([here[:BLOCK], tile(there, 1, 1).T], axis=1)
    low = jnp.concatenate([tile(here, 0, 1).T, here[BLOCK:]], axis=1)
    return jnp.concatenate([top, low], axis=0)


VMEM_SPEC = pl.BlockSpec(memory_space=pltpu.VMEM)
SMEM_SPEC = pl.BlockSpec(memory_space=pltpu.SMEM)


def f32(*shape):
    return jax.ShapeDtypeStruct(shape, jnp.float32)


def call(kernel, out_shape, scalars, arrays, flops):
    many = isinstance(out_shape, (list, tuple))
    moved = sum(a.size * a.dtype.itemsize for a in arrays)
    return pl.pallas_call(
        kernel,
        out_shape=out_shape,
        in_specs=[SMEM_SPEC] * len(scalars) + [VMEM_SPEC] * len(arrays),
        out_specs=[VMEM_SPEC] * len(out_shape) if many else VMEM_SPEC,
        compiler_params=pltpu.CompilerParams(vmem_limit_bytes=16 << 20),
        cost_estimate=pl.CostEstimate(flops=flops, bytes_accessed=moved, transcendentals=0),
    )(*scalars, *arrays)


def as_column(row):
    n = row.shape[1]
    eye = lax.broadcasted_iota(jnp.int32, (n, n), 0) == lax.broadcasted_iota(jnp.int32, (n, n), 1)
    return jnp.sum(jnp.where(eye, row, 0.0), axis=1, keepdims=True)


def partial_kernel(flags, pattern, factor, ramp, hess, mine, theirs, image, ramp_rows):
    step = pl.program_id(0)
    chunk = ramp.shape[1]
    blocks = chunk // BLOCK
    masked = jnp.concatenate(
        [
            jnp.where(
                pattern[0, 0, step * blocks + b] != 0,
                factor[0, 0, b * BLOCK : (b + 1) * BLOCK, :],
                jnp.bfloat16(0),
            )
            for b in range(blocks)
        ],
        axis=0,
    )
    here = lax.dot_general(masked, ramp[0], (((0,), (0,)), ((), ())), preferred_element_type=jnp.float32)

    @pl.when(step == 0)
    def _():
        image[...] = here

    @pl.when(step != 0)
    def _():
        image[...] = image[...] + here

    @pl.when(flags[2] // chunk == step)
    def _():
        start = pl.multiple_of(flags[2] - step * chunk, 32)
        ramp_rows[...] = ramp[0, pl.ds(start, 32), :].astype(jnp.float32)

    @pl.when(step == pl.num_programs(0) - 1)
    def _():
        even, core = flags[0] == 0, flags[1]
        half = image.shape[1] // 2
        left = jnp.concatenate([image[...], ramp_rows[...] * as_column(hess[...])], axis=0)
        right = jnp.concatenate([image[...], ramp_rows[...]], axis=0)
        inner_left = pick(even, left[:, half:], left[:, :half])
        inner_right = pick(even, right[:, half:], right[:, :half])
        outer_left = pick(even, left[:, :half], left[:, half:])
        outer_right = pick(even, right[:, :half], right[:, half:])
        for out, q in ((mine, core), (theirs, 1 - core)):
            inner_half = turned(q == 1, inner_left)[:, : half // 2]
            outer_half = turned(q == 1, outer_left)[:, : half // 2]
            out[:, :384] = cut(tmm(inner_half, turned(q == 1, inner_right)))
            out[:, 384:896] = tmm(inner_half, outer_right)
            out[:, 896:] = cut(tmm(outer_half, turned(q == 1, outer_right)))


def partial(flags, pattern, factors, ramp_map, hess):
    _, _, nv, depth = factors.shape
    iface = ramp_map.shape[2]
    chunk = nv // 4
    return pl.pallas_call(
        partial_kernel,
        grid=(nv // chunk,),
        out_shape=[f32(256, 1280)] * 2,
        in_specs=[
            SMEM_SPEC,
            SMEM_SPEC,
            pl.BlockSpec((1, 1, chunk, depth), lambda i: (0, 0, i, 0)),
            pl.BlockSpec((1, chunk, iface), lambda i: (0, i, 0)),
            pl.BlockSpec(hess.shape, lambda i: (0, 0)),
        ],
        out_specs=[pl.BlockSpec((256, 1280), lambda i: (0, 0))] * 2,
        scratch_shapes=[pltpu.VMEM((depth, iface), jnp.float32), pltpu.VMEM((32, iface), jnp.float32)],
        compiler_params=pltpu.CompilerParams(vmem_limit_bytes=60 << 20),
        cost_estimate=pl.CostEstimate(flops=1 << 30, bytes_accessed=5 << 20, transcendentals=0),
    )(flags, pattern, factors, ramp_map, hess)


def sweep(k, source, ref):
    size = source.shape[0]
    off = k * BLOCK
    end = off + BLOCK
    inv = invert_block(source[off:end, off:end])
    pieces = [inv]
    if off > 0:
        pieces = [mm(inv, source[off:end, :off])] + pieces
    if end < size:
        pieces = pieces + [mm(inv, source[off:end, end:])]
    rows = jnp.concatenate(pieces, axis=1)
    col_id = lax.broadcasted_iota(jnp.int32, (1, size), 1)
    col_in = (col_id >= off) & (col_id < end)
    for low in range(0, size, BLOCK):
        if low != off:
            here = source[low : low + BLOCK, :]
            ref[low : low + BLOCK, :] = jnp.where(col_in, 0.0, here) - mm(here[:, off:end], rows)
    ref[off:end, :] = rows


def first_sweep_kernel(flags, own, other, o_ref):
    first = flags[1] == 0
    top = pick(first, own[:, :384], other[:, :384])
    low = pick(first, other[:, :384], own[:, :384])
    half = top.shape[0]
    o_ref[:half, :] = full_rows(top, low)
    low_rows = full_rows(low, top)
    o_ref[half:, :half] = low_rows[:, half:]
    o_ref[half:, half:] = low_rows[:, :half]
    sweep(0, o_ref, o_ref)


def inverse(flags, own, other):
    size = 2 * own.shape[0]
    m = call(first_sweep_kernel, f32(size, size), [flags], [own, other], 1 << 33)
    for k in range(1, size // BLOCK):
        m = call(functools.partial(sweep, k), f32(size, size), [], [m], 1 << 33)
    return m


def first_join_kernel(flags, inv, own, other, t_ref, removed):
    first = flags[1] == 0
    mine, theirs = own[:, 384:896], other[:, 384:896]
    near = jnp.concatenate([pick(first, mine, theirs), pick(first, theirs, mine)], axis=0)
    t = mm(inv[...], near)
    t_ref[...] = t
    rows = tmm(turned(flags[1] == 1, near)[:, : near.shape[1] // 2], turned(flags[1] == 1, t))
    removed[...] = cut(rows)


def edge_kernel(flags, inv, t, own, other, c_ref, c_half, base):
    core, side = flags[1], flags[3]
    first = core == 0
    width = t.shape[0]
    half = width // 2
    top = pick(first, own[...], other[...])
    low = pick(first, other[...], own[...])
    far = jnp.concatenate([top[:, :width], low[:, :width]], axis=0)
    c = -tmm(far, t[...])
    c_ref[...] = c
    c_half[...] = pick(first, c[:half], c[half:])
    here = pick(side == 0, top[:, width:896], low[:, width:896])
    there = pick(side == 0, low[:, width:896], top[:, width:896])
    edge = turned(side == 1, far)
    rows = full_rows(here, there) - mm(tmm(edge[:, :half], inv[...]), edge)
    base[...] = turned(side == 1, rows)


def last_join_kernel(flags, inv, c, own, other, base, o_ref):
    first, side, early = flags[1] == 0, flags[3], flags[4] == 0
    width = c.shape[0]
    half = width // 2
    z = mm(pick(side == 0, c[:half, :], c[half:, :]), inv[...])
    out_own = base[...] - nt(z, c[...])
    top = -nt(z, pick(first, own[...], other[...]))
    low = -nt(z, pick(first, other[...], own[...]))
    out_other = jnp.concatenate([top, low], axis=1)
    o_ref[:, :width] = pick(early, out_own, out_other)
    o_ref[:, width:] = pick(early, out_other, out_own)


def gram_kernel(flags, f_ref, hess, o_ref):
    core, x_at = flags[1], flags[5]
    both = jnp.concatenate([f_ref[0].astype(jnp.bfloat16), f_ref[1].astype(jnp.bfloat16)], axis=1)
    pieces = []
    for z in range(8):
        here = pl.ds(pl.multiple_of(x_at * 512 + z * 64 + core * 32, 32), 32)
        pieces.append(jnp.concatenate([f_ref[0, here, :], f_ref[1, here, :]], axis=1).astype(jnp.bfloat16))
    lhs = jnp.concatenate(pieces, axis=0)
    total = lax.dot_general(lhs, both, (((1,), (1,)), ((), ())), preferred_element_type=jnp.float32)

    @pl.when(pl.program_id(0) == 0)
    def _():
        o_ref[...] = total

    @pl.when(pl.program_id(0) != 0)
    def _():
        o_ref[...] = o_ref[...] + total

    @pl.when(pl.program_id(0) == pl.num_programs(0) - 1)
    def _():
        own = pl.ds(pl.multiple_of(flags[6] * 32, 32), 32)
        shape = (32, o_ref.shape[1])
        on_diag = lax.broadcasted_iota(jnp.int32, shape, 1) == lax.broadcasted_iota(jnp.int32, shape, 0) + flags[2]
        o_ref[own, :] = o_ref[own, :] + jnp.where(on_diag, as_column(hess[...]), 0.0)


def gram(flags, wide, hess):
    count, nv, depth = wide.shape
    rows = nv // 8
    return pl.pallas_call(
        gram_kernel,
        grid=(count // 2,),
        out_shape=f32(rows, nv),
        in_specs=[
            SMEM_SPEC,
            pl.BlockSpec((2, nv, depth), lambda i: (i, 0, 0)),
            pl.BlockSpec(hess.shape, lambda i: (0, 0)),
        ],
        out_specs=pl.BlockSpec((rows, nv), lambda i: (0, 0)),
        compiler_params=pltpu.CompilerParams(vmem_limit_bytes=16 << 20),
        cost_estimate=pl.CostEstimate(
            flops=2 * count * rows * nv * depth, bytes_accessed=4 * count * nv * depth, transcendentals=0
        ),
    )(flags, wide, hess)


def exchange(v, axes):
    return lax.all_to_all(v, axes, 0, 0, tiled=True)


def rows_sum(v):
    return jnp.sum(exchange(v.reshape(32, v.shape[0] // 32, v.shape[1]), ("x", "z")), axis=0)


def rows_gather(v):
    return exchange(jnp.broadcast_to(v[None], (32,) + v.shape), ("x", "z")).reshape(32 * v.shape[0], v.shape[1])


def tie(v, *others):
    return lax.optimization_barrier((v,) + others)[0]


def other_core(v):
    return lax.ppermute(v, "core", [(0, 1), (1, 0)])


def partner(v, mask):
    return lax.ppermute(v, "period", [(i, i ^ mask) for i in range(4)])


def on_device(factors, pattern, hessian, ramp_map):
    factor = factors[0, 0]
    nv, block_rows = factor.shape
    rows = hessian.shape[1]
    core = lax.axis_index("core")
    x_at = lax.axis_index("x")
    z_at = lax.axis_index("z")
    start = ((x_at * 8 + z_at) * 2 + core) * rows
    period = lax.axis_index("period")
    middle_period = (period == 1) | (period == 2)
    flags = jnp.stack([period % 2, core, start, period % 2, period // 2, x_at, z_at]).astype(jnp.int32)

    with jax.named_scope("interface_partial"):
        mine, theirs = partial(flags, pattern, factors, ramp_map, hessian)
        summed = mine + other_core(theirs)

    with jax.named_scope("schur_gather"):
        present = jnp.repeat(pattern[0, 0], block_rows).astype(jnp.float32)
        factor, present = lax.optimization_barrier((factor, present, summed))[:2]
        wide = lax.optimization_barrier(factor.astype(jnp.float32) * present[:, None])
        wide = lax.all_gather(wide, ("x", "core"))

    with jax.named_scope("interface_sum"):
        total = rows_sum(summed)

    with jax.named_scope("schur_partial"):
        partial_sum = gram(flags, tie(wide, total).reshape(8, nv, block_rows), hessian)

    with jax.named_scope("interface_gather"):
        beside = partner(total, 1)
        near = jnp.where(middle_period, total[:, 384:896], beside[:, 384:896])
        first = rows_gather(jnp.concatenate([total[:, :384] + beside[:, :384], near], axis=1))
        far = jnp.where(middle_period, beside[:, 384:], total[:, 384:])
        kept_outer = jnp.where(middle_period, total[:, 896:], beside[:, 896:])
        kept_outer = kept_outer + partner(kept_outer, 3)
        first = tie(first, partial_sum, kept_outer)
        first_other = other_core(first)
        far = rows_gather(tie(jnp.concatenate([far, kept_outer], axis=1), first))

    with jax.named_scope("first_join"):
        inv1 = inverse(flags, first, first_other)
        t, removed = call(
            first_join_kernel, [f32(512, 512), f32(256, 384)], [flags], [inv1, first, first_other], 1 << 32
        )
        moved = removed + partner(removed, 3)
        far = tie(far, moved)
        far_other = other_core(far)
        kept = far[:, 896:] - moved
        kept_other = other_core(kept)
        c, c_half, base = call(
            edge_kernel, [f32(512, 512), f32(256, 512), f32(256, 512)], [flags], [inv1, t, far, far_other], 1 << 32
        )
        c_half = partner(c_half, 3)
        c_half_other = other_core(c_half)

    with jax.named_scope("schur_sum"):
        schur_rows = lax.psum_scatter(tie(partial_sum, removed), "z", scatter_dimension=0, tiled=True)

    with jax.named_scope("last_join"):
        inv2 = inverse(tie(flags, base), kept, kept_other)
        my_rows = call(last_join_kernel, f32(256, 1024), [flags], [inv2, c, c_half, c_half_other, base], 1 << 31)
    return (schur_rows[None], my_rows)


def solution(mesh):
    fine = Mesh(mesh.devices.reshape(4, 4, 8, 2), ("period",) + CONT_AXES)
    in_specs = (
        P("period", CONT_AXES, None, None),
        P("period", CONT_AXES, None),
        P("period", CONT_AXES),
        P("period", None, None),
    )
    out_specs = (P("period", CONT_AXES, None), P("period", None))
    return jax.shard_map(on_device, mesh=fine, in_specs=in_specs, out_specs=out_specs, check_vma=False)
```

```python
import functools
import jax
import jax.numpy as jnp
from jax import lax
from jax.experimental import pallas as pl
from jax.experimental.pallas import tpu as pltpu
from jax.sharding import Mesh, PartitionSpec as P

HIGHEST = lax.Precision.HIGHEST
BLOCK = 128
PIVOT = 8
CONT_AXES = ("x", "z", "core")


def inverse_2(a, b, d):
    scale = 1.0 / (a * d - b * b)
    return d * scale, -b * scale, a * scale


def inverse_4(s):
    a, b, d = inverse_2(s[0][0], s[0][1], s[1][1])
    q = [[s[i][2], s[i][3]] for i in range(2)]
    t = [[a * q[0][j] + b * q[1][j] for j in range(2)], [b * q[0][j] + d * q[1][j] for j in range(2)]]
    e = s[2][2] - (q[0][0] * t[0][0] + q[1][0] * t[1][0])
    f = s[2][3] - (q[0][0] * t[0][1] + q[1][0] * t[1][1])
    g = s[3][3] - (q[0][1] * t[0][1] + q[1][1] * t[1][1])
    x, y, w = inverse_2(e, f, g)
    u = [[t[i][0] * x + t[i][1] * y, t[i][0] * y + t[i][1] * w] for i in range(2)]
    i00 = a + u[0][0] * t[0][0] + u[0][1] * t[0][1]
    i01 = b + u[0][0] * t[1][0] + u[0][1] * t[1][1]
    i11 = d + u[1][0] * t[1][0] + u[1][1] * t[1][1]
    n = [[-v for v in row] for row in u]
    return [[i00, i01] + n[0], [i01, i11] + n[1], [n[0][0], n[1][0], x, y], [n[0][1], n[1][1], y, w]]


def inverse_8(s):
    span = range(4)
    q = [row[4:] for row in s[:4]]
    corner = inverse_4([row[:4] for row in s[:4]])
    t = [[sum(corner[i][k] * q[k][j] for k in span) for j in span] for i in span]
    rest = [[None] * 4 for _ in span]
    for i in span:
        for j in range(i, 4):
            rest[i][j] = rest[j][i] = s[4 + i][4 + j] - sum(q[k][i] * t[k][j] for k in span)
    low = inverse_4(rest)
    u = [[sum(t[i][k] * low[k][j] for k in span) for j in span] for i in span]
    top = [[None] * 4 for _ in span]
    for i in span:
        for j in range(i, 4):
            top[i][j] = top[j][i] = corner[i][j] + sum(u[i][k] * t[j][k] for k in span)
    return [top[i] + [-v for v in u[i]] for i in span] + [[-u[j][i] for j in span] + low[i] for i in span]


def invert_block(a):
    lane = lax.broadcasted_iota(jnp.int32, (1, BLOCK), 1)
    sub = lax.broadcasted_iota(jnp.int32, (BLOCK, 1), 0)
    span = range(PIVOT)
    for k in range(0, BLOCK, PIVOT):
        rows = [a[k + i : k + i + 1, :] for i in span]
        cols = [a[:, k + i : k + i + 1] for i in span]
        s = [[None] * PIVOT for _ in span]
        for i in span:
            for j in range(i, PIVOT):
                s[i][j] = s[j][i] = jnp.broadcast_to(a[k + i : k + i + 1, k + j : k + j + 1], (1, BLOCK))
        s = inverse_8(s)
        lane_in = (lane >= k) & (lane < k + PIVOT)
        sub_in = (sub >= k) & (sub < k + PIVOT)
        ident = [jnp.where(lane == k + i, 1.0, jnp.where(lane_in, 0.0, rows[i])) for i in span]
        new_rows = [sum(s[i][j] * ident[j] for j in span) for i in span]
        a = jnp.where(lane_in | sub_in, 0.0, a)
        for i in span:
            a = a - jnp.where(sub == k + i, -1.0, jnp.where(sub_in, 0.0, cols[i])) * new_rows[i]
    return a


def mm(a, b):
    return jnp.dot(a, b, precision=HIGHEST, preferred_element_type=jnp.float32)


def tmm(a, b):
    dims = (((0,), (0,)), ((), ()))
    return lax.dot_general(a, b, dims, precision=HIGHEST, preferred_element_type=jnp.float32)


def nt(a, b):
    dims = (((1,), (1,)), ((), ()))
    return lax.dot_general(a, b, dims, precision=HIGHEST, preferred_element_type=jnp.float32)


def pick(first, a, b):
    return jnp.where(first, a, b)


def turned(second, a):
    half = a.shape[1] // 2
    return jnp.where(second, jnp.concatenate([a[:, half:], a[:, :half]], axis=1), a)


def cut(rows):
    return jnp.concatenate([rows[:BLOCK, : 3 * BLOCK], rows[BLOCK:, BLOCK:]], axis=0)


def tile(half, row, place):
    return half[row * BLOCK : (row + 1) * BLOCK, place * BLOCK : (place + 1) * BLOCK]


def full_rows(here, there):
    top = jnp.concatenate([here[:BLOCK], tile(there, 1, 1).T], axis=1)
    low = jnp.concatenate([tile(here, 0, 1).T, here[BLOCK:]], axis=1)
    return jnp.concatenate([top, low], axis=0)


VMEM_SPEC = pl.BlockSpec(memory_space=pltpu.VMEM)
SMEM_SPEC = pl.BlockSpec(memory_space=pltpu.SMEM)


def f32(*shape):
    return jax.ShapeDtypeStruct(shape, jnp.float32)


def call(kernel, out_shape, scalars, arrays, flops):
    many = isinstance(out_shape, (list, tuple))
    moved = sum(a.size * a.dtype.itemsize for a in arrays)
    return pl.pallas_call(
        kernel,
        out_shape=out_shape,
        in_specs=[SMEM_SPEC] * len(scalars) + [VMEM_SPEC] * len(arrays),
        out_specs=[VMEM_SPEC] * len(out_shape) if many else VMEM_SPEC,
        compiler_params=pltpu.CompilerParams(vmem_limit_bytes=16 << 20),
        cost_estimate=pl.CostEstimate(flops=flops, bytes_accessed=moved, transcendentals=0),
    )(*scalars, *arrays)


def as_column(row):
    n = row.shape[1]
    eye = lax.broadcasted_iota(jnp.int32, (n, n), 0) == lax.broadcasted_iota(jnp.int32, (n, n), 1)
    return jnp.sum(jnp.where(eye, row, 0.0), axis=1, keepdims=True)


def partial_kernel(flags, pattern, factor, ramp, hess, mine, theirs, image, ramp_rows):
    step = pl.program_id(0)
    chunk = ramp.shape[1]
    blocks = chunk // BLOCK
    masked = jnp.concatenate(
        [
            jnp.where(
                pattern[0, 0, step * blocks + b] != 0,
                factor[0, 0, b * BLOCK : (b + 1) * BLOCK, :],
                jnp.bfloat16(0),
            )
            for b in range(blocks)
        ],
        axis=0,
    )
    here = lax.dot_general(masked, ramp[0], (((0,), (0,)), ((), ())), preferred_element_type=jnp.float32)

    @pl.when(step == 0)
    def _():
        image[...] = here

    @pl.when(step != 0)
    def _():
        image[...] = image[...] + here

    @pl.when(flags[2] // chunk == step)
    def _():
        start = pl.multiple_of(flags[2] - step * chunk, 32)
        ramp_rows[...] = ramp[0, pl.ds(start, 32), :].astype(jnp.float32)

    @pl.when(step == pl.num_programs(0) - 1)
    def _():
        even, core = flags[0] == 0, flags[1]
        half = image.shape[1] // 2
        left = jnp.concatenate([image[...], ramp_rows[...] * as_column(hess[...])], axis=0)
        right = jnp.concatenate([image[...], ramp_rows[...]], axis=0)
        inner_left = pick(even, left[:, half:], left[:, :half])
        inner_right = pick(even, right[:, half:], right[:, :half])
        outer_left = pick(even, left[:, :half], left[:, half:])
        outer_right = pick(even, right[:, :half], right[:, half:])
        for out, q in ((mine, core), (theirs, 1 - core)):
            inner_half = turned(q == 1, inner_left)[:, : half // 2]
            outer_half = turned(q == 1, outer_left)[:, : half // 2]
            out[:, :384] = cut(tmm(inner_half, turned(q == 1, inner_right)))
            out[:, 384:896] = tmm(inner_half, outer_right)
            out[:, 896:] = cut(tmm(outer_half, turned(q == 1, outer_right)))


def partial(flags, pattern, factors, ramp_map, hess):
    _, _, nv, depth = factors.shape
    iface = ramp_map.shape[2]
    chunk = nv // 4
    return pl.pallas_call(
        partial_kernel,
        grid=(nv // chunk,),
        out_shape=[f32(256, 1280)] * 2,
        in_specs=[
            SMEM_SPEC,
            SMEM_SPEC,
            pl.BlockSpec((1, 1, chunk, depth), lambda i: (0, 0, i, 0)),
            pl.BlockSpec((1, chunk, iface), lambda i: (0, i, 0)),
            pl.BlockSpec(hess.shape, lambda i: (0, 0)),
        ],
        out_specs=[pl.BlockSpec((256, 1280), lambda i: (0, 0))] * 2,
        scratch_shapes=[pltpu.VMEM((depth, iface), jnp.float32), pltpu.VMEM((32, iface), jnp.float32)],
        compiler_params=pltpu.CompilerParams(vmem_limit_bytes=60 << 20),
        cost_estimate=pl.CostEstimate(flops=1 << 30, bytes_accessed=5 << 20, transcendentals=0),
    )(flags, pattern, factors, ramp_map, hess)


def sweep(k, source, inv, ref):
    size = source.shape[0]
    off = k * BLOCK
    end = off + BLOCK
    pieces = [inv]
    if off > 0:
        pieces = [mm(inv, source[off:end, :off])] + pieces
    if end < size:
        pieces = pieces + [mm(inv, source[off:end, end:])]
    rows = jnp.concatenate(pieces, axis=1)
    col_id = lax.broadcasted_iota(jnp.int32, (1, size), 1)
    col_in = (col_id >= off) & (col_id < end)
    following = None
    starts = [low for low in range(end, size, BLOCK)] + [low for low in range(0, off, BLOCK)]
    for low in starts:
        here = source[low : low + BLOCK, :]
        changed = jnp.where(col_in, 0.0, here) - mm(here[:, off:end], rows)
        ref[low : low + BLOCK, :] = changed
        if low == end:
            following = invert_block(changed[:, low : low + BLOCK])
    ref[off:end, :] = rows
    return following


def first_sweep_kernel(flags, own, other, o_ref, inv_ref):
    first = flags[1] == 0
    top = pick(first, own[:, :384], other[:, :384])
    low = pick(first, other[:, :384], own[:, :384])
    half = top.shape[0]
    o_ref[:half, :] = full_rows(top, low)
    low_rows = full_rows(low, top)
    o_ref[half:, :half] = low_rows[:, half:]
    o_ref[half:, half:] = low_rows[:, :half]
    inv_ref[...] = sweep(0, o_ref, invert_block(top[:BLOCK, :BLOCK]), o_ref)


def middle_sweep_kernel(k, source, inv, o_ref, inv_ref):
    inv_ref[...] = sweep(k, source, inv[...], o_ref)


def final_sweep_kernel(k, source, inv, o_ref):
    sweep(k, source, inv[...], o_ref)


def inverse(flags, own, other, flops):
    size = 2 * own.shape[0]
    last = size // BLOCK - 1
    shapes = [f32(size, size), f32(BLOCK, BLOCK)]
    m, inv = call(first_sweep_kernel, shapes, [flags], [own, other], flops)
    for k in range(1, last):
        m, inv = call(functools.partial(middle_sweep_kernel, k), shapes, [], [m, inv], flops)
    return call(functools.partial(final_sweep_kernel, last), f32(size, size), [], [m, inv], flops // 4)


def first_join_kernel(flags, inv, own, other, t_ref, removed):
    first = flags[1] == 0
    mine, theirs = own[:, 384:896], other[:, 384:896]
    near = jnp.concatenate([pick(first, mine, theirs), pick(first, theirs, mine)], axis=0)
    t = mm(inv[...], near)
    t_ref[...] = t
    rows = tmm(turned(flags[1] == 1, near)[:, : near.shape[1] // 2], turned(flags[1] == 1, t))
    removed[...] = cut(rows)


def edge_kernel(flags, inv, t, own, other, c_ref, c_half, base):
    core, side = flags[1], flags[3]
    first = core == 0
    width = t.shape[0]
    half = width // 2
    top = pick(first, own[...], other[...])
    low = pick(first, other[...], own[...])
    far = jnp.concatenate([top[:, :width], low[:, :width]], axis=0)
    c = -tmm(far, t[...])
    c_ref[...] = c
    c_half[...] = pick(first, c[:half], c[half:])
    here = pick(side == 0, top[:, width:896], low[:, width:896])
    there = pick(side == 0, low[:, width:896], top[:, width:896])
    edge = turned(side == 1, far)
    rows = full_rows(here, there) - mm(tmm(edge[:, :half], inv[...]), edge)
    base[...] = turned(side == 1, rows)


def last_join_kernel(flags, inv, c, own, other, base, o_ref):
    first, side, early = flags[1] == 0, flags[3], flags[4] == 0
    width = c.shape[0]
    half = width // 2
    z = mm(pick(side == 0, c[:half, :], c[half:, :]), inv[...])
    out_own = base[...] - nt(z, c[...])
    top = -nt(z, pick(first, own[...], other[...]))
    low = -nt(z, pick(first, other[...], own[...]))
    out_other = jnp.concatenate([top, low], axis=1)
    o_ref[:, :width] = pick(early, out_own, out_other)
    o_ref[:, width:] = pick(early, out_other, out_own)


def gram_kernel(flags, f_ref, hess, o_ref):
    core, x_at = flags[1], flags[5]
    both = jnp.concatenate([f_ref[0].astype(jnp.bfloat16), f_ref[1].astype(jnp.bfloat16)], axis=1)
    pieces = []
    for z in range(8):
        here = pl.ds(pl.multiple_of(x_at * 512 + z * 64 + core * 32, 32), 32)
        pieces.append(jnp.concatenate([f_ref[0, here, :], f_ref[1, here, :]], axis=1).astype(jnp.bfloat16))
    lhs = jnp.concatenate(pieces, axis=0)
    total = lax.dot_general(lhs, both, (((1,), (1,)), ((), ())), preferred_element_type=jnp.float32)

    @pl.when(pl.program_id(0) == 0)
    def _():
        o_ref[...] = total

    @pl.when(pl.program_id(0) != 0)
    def _():
        o_ref[...] = o_ref[...] + total

    @pl.when(pl.program_id(0) == pl.num_programs(0) - 1)
    def _():
        own = pl.ds(pl.multiple_of(flags[6] * 32, 32), 32)
        shape = (32, o_ref.shape[1])
        on_diag = lax.broadcasted_iota(jnp.int32, shape, 1) == lax.broadcasted_iota(jnp.int32, shape, 0) + flags[2]
        o_ref[own, :] = o_ref[own, :] + jnp.where(on_diag, as_column(hess[...]), 0.0)


def gram(flags, wide, hess):
    count, nv, depth = wide.shape
    rows = nv // 8
    return pl.pallas_call(
        gram_kernel,
        grid=(count // 2,),
        out_shape=f32(rows, nv),
        in_specs=[
            SMEM_SPEC,
            pl.BlockSpec((2, nv, depth), lambda i: (i, 0, 0)),
            pl.BlockSpec(hess.shape, lambda i: (0, 0)),
        ],
        out_specs=pl.BlockSpec((rows, nv), lambda i: (0, 0)),
        compiler_params=pltpu.CompilerParams(vmem_limit_bytes=16 << 20),
        cost_estimate=pl.CostEstimate(
            flops=2 * count * rows * nv * depth, bytes_accessed=4 * count * nv * depth, transcendentals=0
        ),
    )(flags, wide, hess)


def exchange(v, axes):
    return lax.all_to_all(v, axes, 0, 0, tiled=True)


def rows_sum(v):
    return jnp.sum(exchange(v.reshape(32, v.shape[0] // 32, v.shape[1]), ("x", "z")), axis=0)


def rows_gather(v):
    return exchange(jnp.broadcast_to(v[None], (32,) + v.shape), ("x", "z")).reshape(32 * v.shape[0], v.shape[1])


def tie(v, *others):
    return lax.optimization_barrier((v,) + others)[0]


def other_core(v):
    return lax.ppermute(v, "core", [(0, 1), (1, 0)])


def partner(v, mask):
    return lax.ppermute(v, "period", [(i, i ^ mask) for i in range(4)])


def on_device(factors, pattern, hessian, ramp_map):
    factor = factors[0, 0]
    nv, block_rows = factor.shape
    rows = hessian.shape[1]
    core = lax.axis_index("core")
    x_at = lax.axis_index("x")
    z_at = lax.axis_index("z")
    start = ((x_at * 8 + z_at) * 2 + core) * rows
    period = lax.axis_index("period")
    middle_period = (period == 1) | (period == 2)
    flags = jnp.stack([period % 2, core, start, period % 2, period // 2, x_at, z_at]).astype(jnp.int32)

    with jax.named_scope("interface_partial"):
        mine, theirs = partial(flags, pattern, factors, ramp_map, hessian)
        summed = mine + other_core(theirs)

    with jax.named_scope("schur_gather"):
        present = jnp.repeat(pattern[0, 0], block_rows).astype(jnp.float32)
        factor, present = lax.optimization_barrier((factor, present, summed))[:2]
        wide = lax.optimization_barrier(factor.astype(jnp.float32) * present[:, None])
        wide = lax.all_gather(wide, ("x", "core"))

    with jax.named_scope("interface_sum"):
        total = rows_sum(summed)

    with jax.named_scope("schur_partial"):
        partial_sum = gram(flags, tie(wide, total).reshape(8, nv, block_rows), hessian)

    with jax.named_scope("interface_gather"):
        beside = partner(total, 1)
        near = jnp.where(middle_period, total[:, 384:896], beside[:, 384:896])
        first = rows_gather(jnp.concatenate([total[:, :384] + beside[:, :384], near], axis=1))
        far = jnp.where(middle_period, beside[:, 384:], total[:, 384:])
        kept_outer = jnp.where(middle_period, total[:, 896:], beside[:, 896:])
        kept_outer = kept_outer + partner(kept_outer, 3)
        first = tie(first, partial_sum, kept_outer)
        first_other = other_core(first)
        far = rows_gather(tie(jnp.concatenate([far, kept_outer], axis=1), first))

    with jax.named_scope("first_join"):
        inv1 = inverse(flags, first, first_other, 1 << 33)
        t, removed = call(
            first_join_kernel, [f32(512, 512), f32(256, 384)], [flags], [inv1, first, first_other], 1 << 32
        )
        moved = removed + partner(removed, 3)
        far = tie(far, moved)
        far_other = other_core(far)
        kept = far[:, 896:] - moved
        kept_other = other_core(kept)
        c, c_half, base = call(
            edge_kernel, [f32(512, 512), f32(256, 512), f32(256, 512)], [flags], [inv1, t, far, far_other], 1 << 32
        )
        c_half = partner(c_half, 3)
        c_half_other = other_core(c_half)

    with jax.named_scope("schur_sum"):
        schur_rows = lax.psum_scatter(tie(partial_sum, removed), "z", scatter_dimension=0, tiled=True)

    with jax.named_scope("last_join"):
        inv2 = inverse(tie(flags, base), kept, kept_other, 3 << 31)
        my_rows = call(last_join_kernel, f32(256, 1024), [flags], [inv2, c, c_half, c_half_other, base], 1 << 31)
    return (schur_rows[None], my_rows)


def solution(mesh):
    fine = Mesh(mesh.devices.reshape(4, 4, 8, 2), ("period",) + CONT_AXES)
    in_specs = (
        P("period", CONT_AXES, None, None),
        P("period", CONT_AXES, None),
        P("period", CONT_AXES),
        P("period", None, None),
    )
    out_specs = (P("period", CONT_AXES, None), P("period", None))
    return jax.shard_map(on_device, mesh=fine, in_specs=in_specs, out_specs=out_specs, check_vma=False)
```
